512 devices in a mesh: grid: 16 (over z_hi, x, core), comp: 32 (over y, z_lo).
Axes of the slice: x: 4, y: 8, z: 8 (z_hi: 2, z_lo: 4; z = z_hi * 4 + z_lo), core: 2. Of those that a mesh axis runs over, the one named last changes fastest.
Arguments:
- spectra: float32 [32, 32, 36, 8192], P('comp', None, None, 'grid'), may hold values from 0.1 to 2
- u_wind: float32 [32, 8192], P(None, 'grid'), may hold values from 2 to 20
- wind_dir: float32 [32, 8192], P(None, 'grid'), may hold values from -3.140625 to 3.140625
- sea_mask: int32 [32, 8192], P(None, 'grid'), may hold values from 0 to 1, as said below
Outputs:
- spectra_next: float32 [32, 32, 36, 8192], P('comp', None, None, 'grid')
The draws below stay inside these ranges and needn't reach their ends.
Inputs may be any that keep to these rules, and one draw needn't show every extreme that they name: sea_mask is 1 at sea and 0 on land; land lies in rectangular blocks of rows and columns.
All inputs are finite; a program needn't handle non-finite values.
Results may differ from the reference program's by a relative error of at most 0.00016.
Values sent between devices are 32-bit elements; how exact they have to be, the bound alone decides.
A program may use at most 64 MiB of HBM per device.

```python
import math
import jax
import jax.numpy as jnp
from jax import lax

NK = 32
NTH = 36
LAT = 32
NLON = 8192


def draw_sea_mask(key, part):
    block_count = max(4, NLON // 16)
    keys = jax.random.split(key, 4)
    top_row = jax.random.randint(keys[0], (block_count, 1, 1), 0, LAT)
    height = jax.random.randint(keys[1], (block_count, 1, 1), 2, LAT // 2 + 3)
    left_col = jax.random.randint(keys[2], (block_count, 1, 1), 0, NLON)
    breadth = jax.random.randint(keys[3], (block_count, 1, 1), 3, 41)
    row_index = jnp.arange(LAT, dtype=jnp.int32)[None, :, None]
    col_index = jnp.arange(NLON, dtype=jnp.int32)[None, None, :]
    inside = (row_index >= top_row) & (row_index < top_row + height) & (col_index >= left_col) & (col_index < left_col + breadth)
    land_cells = jnp.any(inside, axis=0)
    return jnp.where(land_cells, 0, 1).astype(jnp.int32)


def block_scale(key, shape, cuts, low, high):
    level, own = 1.0, jax.random.fold_in(key, 6)
    for axis_at, blocks in cuts:
        heights = jnp.exp(jax.random.uniform(jax.random.fold_in(own, axis_at), (blocks,), jnp.float32, low / len(cuts), high / len(cuts)))
        level = level * jnp.repeat(heights, shape[axis_at] // blocks).reshape([-1 if axis == axis_at else 1 for axis in range(len(shape))])
    return level


def setup_inputs(seed: int = 0) -> dict:
    streams_of = jax.random.split(jax.random.key(seed), 5)
    return {
        "spectra": jnp.clip(jnp.exp(math.log(2.0) - 2.9957323 * jax.random.uniform(streams_of[0], (NK, LAT, NTH, NLON), jnp.float32) ** block_scale(streams_of[0], (NK, LAT, NTH, NLON), ((0, 32), (3, 16)), -0.2, 0.2)), 0.1, 2.0),
        "u_wind": jnp.clip(2.0 + 18.0 * jax.random.uniform(streams_of[1], (LAT, NLON), jnp.float32) ** block_scale(streams_of[1], (LAT, NLON), ((1, 16),), -0.2, 0.2), 2.0, 20.0),
        "wind_dir": jnp.clip(jax.random.uniform(streams_of[2], (LAT, NLON), jnp.float32, -3.140625, 3.140625), -3.140625, 3.140625),
        "sea_mask": draw_sea_mask(jax.random.fold_in(streams_of[4], 71), 0),
    }


GRAVITY = 9.81
FREQ_LOW = 0.04
FREQ_RATIO = 1.1
LAMBDA = 0.25
SOURCE_STEP = 120.0
ADVECT_STEP = 220.0
WIND_FACTOR = 3.125e-4
TRANSFER_FACTOR = 0.1
EARTH_RADIUS = 6.371e6
BAND_CENTRE = 30.0
CELL_DEGREES = 0.05
CELL_RADIANS = CELL_DEGREES * math.pi / 180.0
ANGLE_NEAR = 11.48
ANGLE_FAR = 33.56
FREQ_UPPER_SHIFT = math.log(1.0 + LAMBDA) / math.log(FREQ_RATIO)
FREQ_LOWER_SHIFT = math.log(1.0 - LAMBDA) / math.log(FREQ_RATIO)
WEIGHT_UPPER = 1.0 / (1.0 + LAMBDA) ** 4
WEIGHT_LOWER = 1.0 / (1.0 - LAMBDA) ** 4
WEIGHT_CROSS = 2.0 / (1.0 - LAMBDA * LAMBDA) ** 4
HIGHEST = lax.Precision.HIGHEST


def hat_matrix(bin_count, bin_shift, periodic):
    target = jnp.arange(bin_count, dtype=jnp.float32)[:, None] + bin_shift
    source = jnp.arange(bin_count, dtype=jnp.float32)[None, :]
    offset_gap = target - source
    if periodic:
        offset_gap = jnp.mod(offset_gap + bin_count / 2.0, float(bin_count)) - bin_count / 2.0
    return jnp.maximum(0.0, 1.0 - jnp.abs(offset_gap))


def nonlinear(point_block):
    freq_count = point_block.shape[0]
    dir_count = point_block.shape[2]
    freq_upper = hat_matrix(freq_count, FREQ_UPPER_SHIFT, False)
    freq_lower = hat_matrix(freq_count, FREQ_LOWER_SHIFT, False)
    spread_upper = jnp.einsum("km,mrjq->krjq", freq_upper, point_block, precision=HIGHEST)
    spread_lower = jnp.einsum("km,mrjq->krjq", freq_lower, point_block, precision=HIGHEST)
    near_bins = ANGLE_NEAR * dir_count / 360.0
    far_bins = ANGLE_FAR * dir_count / 360.0
    squared = point_block * point_block
    centre_total = jnp.zeros_like(point_block)
    back_upper = jnp.zeros_like(point_block)
    back_lower = jnp.zeros_like(point_block)
    for shifts in ((near_bins, -far_bins), (-near_bins, far_bins)):
        dir_upper = hat_matrix(dir_count, shifts[0], True)
        dir_lower = hat_matrix(dir_count, shifts[1], True)
        plus_value = jnp.einsum("jn,krnq->krjq", dir_upper, spread_upper, precision=HIGHEST)
        minus_value = jnp.einsum("jn,krnq->krjq", dir_lower, spread_lower, precision=HIGHEST)
        interaction = TRANSFER_FACTOR * (squared * (plus_value * WEIGHT_UPPER + minus_value * WEIGHT_LOWER)
                                         - WEIGHT_CROSS * point_block * plus_value * minus_value)
        centre_total = centre_total - 2.0 * interaction
        back_upper = back_upper + jnp.einsum("jn,krjq->krnq", dir_upper, interaction, precision=HIGHEST)
        back_lower = back_lower + jnp.einsum("jn,krjq->krnq", dir_lower, interaction, precision=HIGHEST)
    centre_total = centre_total + jnp.einsum("km,krjq->mrjq", freq_upper, back_upper, precision=HIGHEST)
    return centre_total + jnp.einsum("km,krjq->mrjq", freq_lower, back_lower, precision=HIGHEST)


def frequency(freq_index):
    return (FREQ_LOW * jnp.power(FREQ_RATIO, freq_index.astype(jnp.float32))).reshape(-1, 1, 1, 1)


def wind_growth(freq, angles, wind_speed, heading):
    radian_freq = 2.0 * math.pi * freq
    celerity = GRAVITY / radian_freq
    alignment = jnp.cos(angles) * jnp.cos(heading) + jnp.sin(angles) * jnp.sin(heading)
    return WIND_FACTOR * SOURCE_STEP * radian_freq * jnp.maximum(0.0, wind_speed / celerity * alignment - 1.0)


def courant_x(freq, angles, row_index, total_rows):
    group_speed = GRAVITY / (4.0 * math.pi * freq)
    latitude = BAND_CENTRE + (row_index.astype(jnp.float32) - (total_rows - 1) / 2.0) * CELL_DEGREES
    row_cos = jnp.cos(latitude * (math.pi / 180.0)).reshape(1, -1, 1, 1)
    return group_speed * jnp.cos(angles) * ADVECT_STEP / (EARTH_RADIUS * row_cos * CELL_RADIANS)


def courant_y(freq, angles):
    group_speed = GRAVITY / (4.0 * math.pi * freq)
    return group_speed * jnp.sin(angles) * ADVECT_STEP / (EARTH_RADIUS * CELL_RADIANS)


def latitude_cos(total_rows):
    cell_lat = BAND_CENTRE + (jnp.arange(total_rows, dtype=jnp.float32) - (total_rows - 1) / 2.0) * CELL_DEGREES
    face_lat = BAND_CENTRE + (jnp.arange(total_rows + 1, dtype=jnp.float32) - total_rows / 2.0) * CELL_DEGREES
    cell_cos = jnp.cos(cell_lat * (math.pi / 180.0)).reshape(1, -1, 1, 1)
    face_cos = jnp.cos(face_lat * (math.pi / 180.0)).reshape(1, -1, 1, 1)
    return face_cos, 1.0 / cell_cos


def advect(padded, courant, face_weight, cell_weight, along_axis):
    cells = padded.shape[along_axis] - 4

    def piece_at(offset_cells, length_cells):
        return lax.slice_in_dim(padded, offset_cells, offset_cells + length_cells, axis=along_axis)

    left_cell = piece_at(1, cells + 1)
    right_cell = piece_at(2, cells + 1)
    far_left = piece_at(0, cells + 1)
    far_right = piece_at(3, cells + 1)
    curvature = jnp.where(courant >= 0.0, right_cell - 2.0 * left_cell + far_left,
                          far_right - 2.0 * right_cell + left_cell)
    face_value = 0.5 * (left_cell + right_cell) - 0.5 * courant * (right_cell - left_cell) \
        - (1.0 - courant * courant) / 6.0 * curvature
    flux_face = courant * face_value * face_weight
    difference = lax.slice_in_dim(flux_face, 1, cells + 1, axis=along_axis) - lax.slice_in_dim(flux_face, 0, cells, axis=along_axis)
    return piece_at(2, cells) - difference * cell_weight


def reference(spectra, u_wind, wind_dir, sea_mask):
    mask_field = sea_mask.astype(jnp.float32)[None, :, None, :]
    masked = spectra * mask_field
    freq = frequency(jnp.arange(NK, dtype=jnp.int32))
    angles = (jnp.arange(NTH, dtype=jnp.float32) * (2.0 * math.pi / NTH)).reshape(1, 1, -1, 1)
    growth = wind_growth(freq, angles, u_wind[None, :, None, :], wind_dir[None, :, None, :])
    block_width = math.gcd(NLON, 256)
    block_total = NLON // block_width
    stacked = jnp.moveaxis(masked.reshape(NK, LAT, NTH, block_total, block_width), 3, 0)
    pieces = lax.map(nonlinear, stacked)
    increment = jnp.moveaxis(pieces, 0, 3).reshape(NK, LAT, NTH, NLON)
    post = masked * (1.0 + growth) + increment
    padded = jnp.pad(post, ((0, 0), (0, 0), (0, 0), (2, 2)))
    crossing = courant_x(freq, angles, jnp.arange(LAT, dtype=jnp.int32), LAT)
    swept_x = advect(padded, crossing, 1.0, 1.0, 3) * mask_field
    padded_rows = jnp.pad(swept_x, ((0, 0), (2, 2), (0, 0), (0, 0)))
    face_cos, cell_inverse = latitude_cos(LAT)
    return advect(padded_rows, courant_y(freq, angles), face_cos, cell_inverse, 1) * mask_field
```

```python
import math

import numpy as np

import jax
import jax.numpy as jnp
from jax import lax
from jax.experimental import pallas as pl
from jax.experimental.pallas import tpu as pltpu
from jax.sharding import PartitionSpec as P

MESH = pl.DeviceIdType.MESH
NK, NTH, LAT = 32, 36, 32
GRAVITY = 9.81
LAMBDA = 0.25
WIND = 0.0003125 * 120.0
ADVECT_STEP = 220.0
EARTH_RADIUS = 6371000.0
BAND_CENTRE = 30.0
CELL_DEGREES = 0.05
CELL_RADIANS = CELL_DEGREES * math.pi / 180.0
SHIFT_UP = math.log(1.0 + LAMBDA) / math.log(1.1)
SHIFT_DOWN = math.log(1.0 - LAMBDA) / math.log(1.1)
NEAR = 11.48 * NTH / 360.0
FAR = 33.56 * NTH / 360.0
U1 = SHIFT_UP - 2.0
U0 = 1.0 - U1
D1W = -SHIFT_DOWN - 3.0
D0W = 1.0 - D1W
N1 = NEAR - 1.0
N0 = 1.0 - N1
F1 = FAR - 3.0
F0 = 1.0 - F1
W_UP = 0.1 / (1.0 + LAMBDA) ** 4
W_DOWN = 0.1 / (1.0 - LAMBDA) ** 4
W_CROSS = 0.2 / (1.0 - LAMBDA * LAMBDA) ** 4

ORDER = (0, 3, 1, 2)
LANES = 128
JB = 4
PAD = 4


def tables():
    t = np.zeros((8, 128), np.float64)
    th = 2.0 * np.pi * np.arange(NTH) / NTH
    t[0, :NTH] = np.cos(th)
    t[1, :NTH] = np.sin(th)
    f = 0.04 * 1.1 ** np.arange(NK)
    w = 2.0 * np.pi * f
    t[2, :NK] = WIND * w
    t[3, :NK] = w / GRAVITY
    t[4, :NK] = GRAVITY / (2.0 * w) * ADVECT_STEP / (EARTH_RADIUS * CELL_RADIANS)
    i = np.arange(LAT)
    cell = np.cos(np.radians(BAND_CENTRE + (i - (LAT - 1) / 2.0) * CELL_DEGREES))
    upper = np.cos(np.radians(BAND_CENTRE + (i + 1 - LAT / 2.0) * CELL_DEGREES))
    lower = np.cos(np.radians(BAND_CENTRE + (i - LAT / 2.0) * CELL_DEGREES))
    t[5, :LAT] = upper / cell
    t[6, :LAT] = lower / cell
    return t.astype(np.float32)


def kernel(
    tab, x_hbm, uw, wd, mk, o_hbm,
    xbuf, obuf, sbuf, ebuf, tbuf, above, below, incr, ibuf, post,
    eux, edx, d1x, d2x, bus, bds, cen, swept, ybuf, taps, rowinv,
    pack_l, pack_r, halo_l, halo_r,
    load_s, store_s, zin_s, zin_r, hal_s, hal_r, bak_s, bak_r, zout_s, zout_r, lon_s, lon_r,
):
    f32 = jnp.float32
    me = lax.axis_index("comp")
    g = lax.axis_index("grid")
    y, z = me // 4, lax.rem(me, 4)
    y_up = lax.rem(y + 1, 8) * 4 + z
    y_dn = lax.rem(y + 7, 8) * 4 + z
    g_right, g_left = lax.rem(g + 1, 16), lax.rem(g + 15, 16)
    has_lo = jnp.where(y > 0, 1.0, 0.0).astype(f32)
    has_hi = jnp.where(y < 7, 1.0, 0.0).astype(f32)
    has_left = jnp.where(g > 0, 1.0, 0.0).astype(f32)
    has_right = jnp.where(g < 15, 1.0, 0.0).astype(f32)

    def zpeer(dz):
        return lax.rem(z + dz, 4)

    def zfrom(dz):
        return lax.rem(z + 4 - dz, 4)

    def load(i):
        return pltpu.make_async_copy(
            x_hbm.at[0, :, :, pl.ds(ORDER[i] * LANES, LANES)], xbuf.at[i], load_s.at[i]
        )

    def store(i):
        return pltpu.make_async_copy(
            obuf.at[i], o_hbm.at[0, :, :, pl.ds(ORDER[i] * LANES, LANES)], store_s.at[i]
        )

    def remote(src, dst, ss, rs, **to):
        return pltpu.make_async_remote_copy(
            src_ref=src, dst_ref=dst, send_sem=ss, recv_sem=rs, device_id=to, device_id_type=MESH
        )

    def zin(i, dz):
        p = zpeer(dz)
        k = i * 4 + dz
        return remote(sbuf.at[i, p], ebuf.at[i, 4 + z], zin_s.at[k], zin_r.at[k], comp=y * 4 + p)

    def hal_up(i, f):
        k = i * 8 + f
        return remote(ebuf.at[i, 4 + f], ebuf.at[i, f], hal_s.at[k], hal_r.at[k], comp=y_up)

    def hal_dn(i, f):
        k = i * 8 + 4 + f
        return remote(ebuf.at[i, 4 + f], ebuf.at[i, 8 + f], hal_s.at[k], hal_r.at[k], comp=y_dn)

    def bak_dn(i, m):
        k = i * 8 + m
        return remote(tbuf.at[i, m], above.at[i, m], bak_s.at[k], bak_r.at[k], comp=y_dn)

    def bak_up(i, m):
        k = i * 8 + 4 + m
        return remote(tbuf.at[i, 8 + m], below.at[i, m], bak_s.at[k], bak_r.at[k], comp=y_up)

    def zout(i, dz):
        p = zpeer(dz)
        k = i * 4 + dz
        return remote(incr.at[i, p], ibuf.at[i, z], zout_s.at[k], zout_r.at[k], comp=y * 4 + p)

    def lon_to_right():
        return remote(pack_r, halo_l, lon_s.at[0], lon_r.at[0], grid=g_right)

    def lon_to_left():
        return remote(pack_l, halo_r, lon_s.at[1], lon_r.at[1], grid=g_left)

    for i in range(4):
        load(i).start()

    barrier = pltpu.get_barrier_semaphore()
    for dz in (1, 2, 3):
        pl.semaphore_signal(barrier, inc=1, device_id={"comp": y * 4 + zpeer(dz)}, device_id_type=MESH)
    pl.semaphore_signal(barrier, inc=1, device_id={"comp": y_up}, device_id_type=MESH)
    pl.semaphore_signal(barrier, inc=1, device_id={"comp": y_dn}, device_id_type=MESH)
    pl.semaphore_signal(barrier, inc=1, device_id={"grid": g_right}, device_id_type=MESH)
    pl.semaphore_signal(barrier, inc=1, device_id={"grid": g_left}, device_id_type=MESH)

    def lanes(i):
        return slice(ORDER[i] * LANES, (ORDER[i] + 1) * LANES)

    def rows8(rg):
        return pl.ds(pl.multiple_of(rg * 8, 8), 8)

    def prepare(i):
        load(i).wait()
        for dz in (2, 1, 3, 0):
            rg = zpeer(dz)
            piece = jnp.swapaxes(xbuf[i, rows8(rg)], 0, 1)
            piece = piece * mk[rows8(rg), lanes(i)].astype(f32)[None]
            sbuf[i, rg] = piece
            if dz == 0:
                ebuf[i, 4 + z] = piece
            else:
                if i == 0 and dz == 2:
                    pl.semaphore_wait(barrier, 7)
                zin(i, dz).start()

    wind_w = tab[2, me]
    inv_cel = tab[3, me]
    courant = tab[4, me]

    def grow(i):
        for rg in range(4):
            speed = uw[rg * 8 : rg * 8 + 8, lanes(i)] * inv_cel
            head = wd[rg * 8 : rg * 8 + 8, lanes(i)]
            along, across = speed * jnp.cos(head), speed * jnp.sin(head)

            @pl.loop(0, NTH, unroll=4)
            def _(j):
                growth = wind_w * jnp.maximum(0.0, tab[0, j] * along + tab[1, j] * across - 1.0)
                post[i, rg, j] = sbuf[i, rg, j] * (1.0 + growth)

    def constants():
        row = lax.broadcasted_iota(jnp.int32, (LAT, LANES), 0).astype(f32)
        lat = BAND_CENTRE + (row - (LAT - 1) / 2.0) * CELL_DEGREES
        rowinv[...] = 1.0 / jnp.cos(lat * (math.pi / 180.0))
        j = lax.broadcasted_iota(jnp.int32, (NTH, LANES), 0).astype(f32)
        c = courant * jnp.sin(j * (2.0 * math.pi / NTH))
        q = (1.0 - c * c) / 6.0
        pos = c >= 0.0
        taps[0] = c * jnp.where(pos, -q, 0.0)
        taps[1] = c * (0.5 + 0.5 * c + jnp.where(pos, 2.0 * q, -q))
        taps[2] = c * (0.5 - 0.5 * c + jnp.where(pos, -q, 2.0 * q))
        taps[3] = c * jnp.where(pos, 0.0, -q)
        for i in range(4):
            below[i, 3] = jnp.zeros((NTH, 8, LANES), f32)
        ybuf[0:2] = jnp.zeros((2, NTH, LANES), f32)
        ybuf[LAT + 2 : LAT + 4] = jnp.zeros((2, NTH, LANES), f32)

    def forward(i):
        for dz in range(4):
            f = zfrom(dz)
            if dz:
                zin(i, dz).wait_recv()
            hal_up(i, f).start()

            @pl.when(f < 3)
            def _():
                hal_dn(i, f).start()

    def interact(i):
        for f in range(4):
            hal_up(i, f).wait_recv()
        for f in range(3):
            hal_dn(i, f).wait_recv()

        @pl.loop(0, 4)
        def _(k):
            lo_a = jnp.where(k < 4, has_lo, 1.0) * D1W
            lo_b = jnp.where(k < 3, has_lo, 1.0) * D0W
            hi_a = jnp.where(k >= 2, has_hi, 1.0) * U0
            hi_b = jnp.where(k >= 1, has_hi, 1.0) * U1

            @pl.loop(0, NTH // JB)
            def _(b):
                at = pl.ds(b * JB, JB)
                to = pl.ds(b * JB + PAD, JB)
                eux[to] = hi_a * ebuf[i, k + 6, at] + hi_b * ebuf[i, k + 7, at]
                edx[to] = lo_b * ebuf[i, k + 1, at] + lo_a * ebuf[i, k, at]

            for ref in (eux, edx):
                ref[0:PAD] = ref[NTH : NTH + PAD]
                ref[NTH + PAD : NTH + 2 * PAD] = ref[PAD : 2 * PAD]

            @pl.loop(0, NTH // JB)
            def _(b):
                def eu(o):
                    return eux[pl.ds(b * JB + PAD + o, JB)]

                def ed(o):
                    return edx[pl.ds(b * JB + PAD + o, JB)]

                e = ebuf[i, k + 4, pl.ds(b * JB, JB)]

                def delta(plus, minus):
                    return e * (e * (W_UP * plus + W_DOWN * minus) - W_CROSS * plus * minus)

                to = pl.ds(b * JB + PAD, JB)
                d1x[to] = delta(N0 * eu(1) + N1 * eu(2), F0 * ed(-3) + F1 * ed(-4))
                d2x[to] = delta(N0 * eu(-1) + N1 * eu(-2), F0 * ed(3) + F1 * ed(4))

            for ref in (d1x, d2x):
                ref[0:PAD] = ref[NTH : NTH + PAD]
                ref[NTH + PAD : NTH + 2 * PAD] = ref[PAD : 2 * PAD]

            @pl.loop(0, NTH // JB)
            def _(b):
                def a1(o):
                    return d1x[pl.ds(b * JB + PAD + o, JB)]

                def a2(o):
                    return d2x[pl.ds(b * JB + PAD + o, JB)]

                at = pl.ds(b * JB, JB)
                bus[k, at] = N0 * (a1(-1) + a2(1)) + N1 * (a1(-2) + a2(2))
                bds[k, at] = F0 * (a1(3) + a2(-3)) + F1 * (a1(4) + a2(-4))
                cen[k, at] = -2.0 * (a1(0) + a2(0))

        @pl.loop(0, NTH)
        def _(j):
            bd = [bds[k, j] for k in range(4)]
            bu = [bus[k, j] for k in range(4)]
            tbuf[i, 0, j] = D1W * bd[0]
            tbuf[i, 1, j] = D0W * bd[0] + D1W * bd[1]
            tbuf[i, 2, j] = D0W * bd[1] + D1W * bd[2]
            tbuf[i, 3, j] = D0W * bd[2] + D1W * bd[3]
            tbuf[i, 4, j] = cen[0, j] + D0W * bd[3]
            tbuf[i, 5, j] = cen[1, j]
            tbuf[i, 6, j] = cen[2, j] + U0 * bu[0]
            tbuf[i, 7, j] = cen[3, j] + U1 * bu[0] + U0 * bu[1]
            tbuf[i, 8, j] = U1 * bu[1] + U0 * bu[2]
            tbuf[i, 9, j] = U1 * bu[2] + U0 * bu[3]
            tbuf[i, 10, j] = U1 * bu[3]

        for m in range(4):
            bak_dn(i, m).start()
            if m < 3:
                bak_up(i, m).start()

    def gather(i):
        for dz in (1, 2, 3, 0):
            m = zpeer(dz)
            bak_dn(i, m).wait_recv()

            @pl.when(m < 3)
            def _():
                bak_up(i, m).wait_recv()

            total = tbuf[i, 4 + m] + has_hi * above[i, m] + has_lo * below[i, m]
            if dz == 0:
                ibuf[i, z] = total
            else:
                incr[i, m] = total
                zout(i, dz).start()

    def finish(i):
        for dz in (1, 2, 3):
            zout(i, dz).wait_recv()

        @pl.loop(0, NTH // JB)
        def _(b):
            at = pl.ds(b * JB, JB)
            for rg in range(4):
                post[i, rg, at] = post[i, rg, at] + ibuf[i, rg, at]

    lane = lax.broadcasted_iota(jnp.int32, (8, LANES), 1)

    def edges():
        first, last = ORDER.index(0), ORDER.index(3)
        for rg in range(4):

            def step(j, acc):
                a, b = acc
                here = (lane == 2 * j) | (lane == 2 * j + 1)
                a = jnp.where(here, pltpu.roll(post[first, rg, j], 2 * j, 1), a)
                b = jnp.where(here, pltpu.roll(post[last, rg, j], 2 * j + 2, 1), b)
                return a, b

            zero = jnp.zeros((8, LANES), f32)
            a, b = lax.fori_loop(0, NTH, step, (zero, zero), unroll=4)
            pack_l[rg] = a
            pack_r[rg] = b
        lon_to_right().start()
        lon_to_left().start()

    def sweep_x(chunks, rg, j, positive, edge_l, edge_r):
        c = (courant * tab[0, j]) * rowinv[rg * 8 : rg * 8 + 8]
        q = (1.0 - c * c) * (1.0 / 6.0)
        one = -q
        if positive:
            mid = 0.5 + 0.5 * c + 2.0 * q
            far = 0.5 - 0.5 * c - q
        else:
            mid = 0.5 - 0.5 * c + 2.0 * q
            far = 0.5 + 0.5 * c - q
        sign = c if positive else -c
        k_next, k_here = sign * far, sign * (mid - far)
        k_back, k_back2 = sign * (one - mid), sign * one
        k_here = 1.0 - k_here
        for col in chunks:
            v = post[ORDER.index(col), rg, j]
            if col == 0:
                vl = edge_l
            else:
                vl = post[ORDER.index(col - 1), rg, j]
            if col == 3:
                vr = edge_r
            else:
                vr = post[ORDER.index(col + 1), rg, j]
            if positive:
                nxt = pltpu.roll(jnp.where(lane == 0, vr, v), LANES - 1, 1)
                back = pltpu.roll(jnp.where(lane == LANES - 1, vl, v), 1, 1)
                back2 = pltpu.roll(jnp.where(lane >= LANES - 2, vl, v), 2, 1)
            else:
                nxt = pltpu.roll(jnp.where(lane == LANES - 1, vl, v), 1, 1)
                back = pltpu.roll(jnp.where(lane == 0, vr, v), LANES - 1, 1)
                back2 = pltpu.roll(jnp.where(lane < 2, vr, v), LANES - 2, 1)
            out = k_here * v - (k_next * nxt + k_back * back - k_back2 * back2)
            swept[ORDER.index(col), rg, j] = out

    def propagate(chunks):
        for rg in range(4):

            @pl.loop(0, NTH // 2)
            def _(t):
                for positive in (True, False):
                    j = lax.rem(t + 27, NTH) if positive else t + 9
                    edge_l = edge_r = None
                    if 0 in chunks:
                        edge_l = has_left * pltpu.roll(halo_l[rg], 126 - 2 * j, 1)
                    if 3 in chunks:
                        edge_r = has_right * pltpu.roll(halo_r[rg], LANES - 2 * j, 1)
                    sweep_x(chunks, rg, j, positive, edge_l, edge_r)

        for col in chunks:
            i = ORDER.index(col)
            for rg in range(4):
                sea = mk[rg * 8 : rg * 8 + 8, lanes(i)].astype(f32)
                ybuf[2 + rg * 8 : 10 + rg * 8] = jnp.swapaxes(swept[i, rg] * sea[None], 0, 1)

            def flux(r):
                return (
                    taps[0] * ybuf[r + 1] + taps[1] * ybuf[r + 2]
                    + taps[2] * ybuf[r + 3] + taps[3] * ybuf[r + 4]
                )

            def rows(block, under):
                sea = mk[rows8(block), lanes(i)].astype(f32)
                for s in range(8):
                    r = block * 8 + s
                    over = flux(r)
                    out = ybuf[r + 2] - (tab[5, r] * over - tab[6, r] * under)
                    obuf[i, r] = out * sea[s : s + 1]
                    under = over
                return under

            first = taps[2] * ybuf[2] + taps[3] * ybuf[3]
            lax.fori_loop(0, LAT // 8, rows, first)
            store(i).start()

    prepare(0)
    prepare(1)
    constants()
    grow(0)
    forward(0)
    prepare(2)
    grow(1)
    forward(1)
    prepare(3)
    interact(0)
    grow(2)
    forward(2)
    interact(1)
    grow(3)
    gather(0)
    forward(3)
    interact(2)
    gather(1)
    interact(3)
    finish(0)
    gather(2)
    finish(1)
    edges()
    gather(3)
    finish(2)
    lon_to_right().wait_recv()
    lon_to_left().wait_recv()
    propagate((0,))
    finish(3)
    propagate((1, 2, 3))

    for i in range(4):
        for dz in (1, 2, 3):
            zin(i, dz).wait_send()
            zout(i, dz).wait_send()
        for f in range(4):
            hal_up(i, f).wait_send()
            bak_dn(i, f).wait_send()
        for f in range(3):
            hal_dn(i, f).wait_send()
            bak_up(i, f).wait_send()
        store(i).wait()
    lon_to_right().wait_send()
    lon_to_left().wait_send()


def shards(spectra, u_wind, wind_dir, sea_mask):
    f32 = jnp.float32
    tile = (NTH, 8, LANES)
    vmem, dma = pltpu.VMEM, pltpu.SemaphoreType.DMA
    inner = pl.BlockSpec(memory_space=pltpu.VMEM)
    return pl.pallas_call(
        kernel,
        out_shape=jax.ShapeDtypeStruct(spectra.shape, f32),
        in_specs=[
            pl.BlockSpec(memory_space=pltpu.SMEM),
            pl.BlockSpec(memory_space=pl.ANY),
            inner, inner, inner,
        ],
        out_specs=pl.BlockSpec(memory_space=pl.ANY),
        scratch_shapes=[
            vmem((4, LAT, NTH, LANES), f32),
            vmem((4, LAT, NTH, LANES), f32),
            vmem((4, 4) + tile, f32),
            vmem((4, 11) + tile, f32),
            vmem((4, 11) + tile, f32),
            vmem((4, 4) + tile, f32),
            vmem((4, 4) + tile, f32),
            vmem((4, 4) + tile, f32),
            vmem((4, 4) + tile, f32),
            vmem((4, 4) + tile, f32),
            vmem((NTH + 2 * PAD, 8, LANES), f32),
            vmem((NTH + 2 * PAD, 8, LANES), f32),
            vmem((NTH + 2 * PAD, 8, LANES), f32),
            vmem((NTH + 2 * PAD, 8, LANES), f32),
            vmem((4,) + tile, f32),
            vmem((4,) + tile, f32),
            vmem((4,) + tile, f32),
            vmem((4, 4) + tile, f32),
            vmem((LAT + 4, NTH, LANES), f32),
            vmem((4, NTH, LANES), f32),
            vmem((LAT, LANES), f32),
            vmem((4, 8, LANES), f32),
            vmem((4, 8, LANES), f32),
            vmem((4, 8, LANES), f32),
            vmem((4, 8, LANES), f32),
            dma((4,)), dma((4,)),
            dma((16,)), dma((16,)),
            dma((32,)), dma((32,)),
            dma((32,)), dma((32,)),
            dma((16,)), dma((16,)),
            dma((2,)), dma((2,)),
        ],
        compiler_params=pltpu.CompilerParams(
            collective_id=0, has_side_effects=True, vmem_limit_bytes=56 << 20
        ),
        cost_estimate=pl.CostEstimate(flops=60_000_000, bytes_accessed=5_000_000, transcendentals=32_768),
        name="wave_step",
    )(tables(), spectra, u_wind, wind_dir, sea_mask)


def solution(mesh):
    return jax.shard_map(
        shards,
        mesh=mesh,
        in_specs=(P("comp", None, None, "grid"), P(None, "grid"), P(None, "grid"), P(None, "grid")),
        out_specs=P("comp", None, None, "grid"),
        check_vma=False,
    )
```

```python
import math

import numpy as np

import jax
import jax.numpy as jnp
from jax import lax
from jax.experimental import pallas as pl
from jax.experimental.pallas import tpu as pltpu
from jax.sharding import PartitionSpec as P

MESH = pl.DeviceIdType.MESH
NK, NTH, LAT = 32, 36, 32
GRAVITY = 9.81
LAMBDA = 0.25
WIND = 0.0003125 * 120.0
ADVECT_STEP = 220.0
EARTH_RADIUS = 6371000.0
BAND_CENTRE = 30.0
CELL_DEGREES = 0.05
CELL_RADIANS = CELL_DEGREES * math.pi / 180.0
SHIFT_UP = math.log(1.0 + LAMBDA) / math.log(1.1)
SHIFT_DOWN = math.log(1.0 - LAMBDA) / math.log(1.1)
NEAR = 11.48 * NTH / 360.0
FAR = 33.56 * NTH / 360.0
U1 = SHIFT_UP - 2.0
U0 = 1.0 - U1
D1W = -SHIFT_DOWN - 3.0
D0W = 1.0 - D1W
N1 = NEAR - 1.0
N0 = 1.0 - N1
F1 = FAR - 3.0
F0 = 1.0 - F1
W_UP = 0.1 / (1.0 + LAMBDA) ** 4
W_DOWN = 0.1 / (1.0 - LAMBDA) ** 4
W_CROSS = 0.2 / (1.0 - LAMBDA * LAMBDA) ** 4

ORDER = (0, 3, 1, 2)
LANES = 128
JB = 4
PAD = 4


def tables():
    t = np.zeros((8, 128), np.float64)
    th = 2.0 * np.pi * np.arange(NTH) / NTH
    t[0, :NTH] = np.cos(th)
    t[1, :NTH] = np.sin(th)
    f = 0.04 * 1.1 ** np.arange(NK)
    w = 2.0 * np.pi * f
    t[2, :NK] = WIND * w
    t[3, :NK] = w / GRAVITY
    t[4, :NK] = GRAVITY / (2.0 * w) * ADVECT_STEP / (EARTH_RADIUS * CELL_RADIANS)
    return t.astype(np.float32)


def kernel(
    tab, x_hbm, uw, wd, mk, o_hbm,
    xbuf, obuf, sbuf, ebuf, tbuf, above, below, incr, ibuf, post,
    eux, edx, d1x, d2x, bus, bds, cen, rowinv, facehi, facelo,
    pack_l, pack_r, halo_l, halo_r,
    load_s, store_s, zin_s, zin_r, hal_s, hal_r, bak_s, bak_r, zout_s, zout_r, lon_s, lon_r,
):
    f32 = jnp.float32
    me = lax.axis_index("comp")
    g = lax.axis_index("grid")
    y, z = me // 4, lax.rem(me, 4)
    y_up = lax.rem(y + 1, 8) * 4 + z
    y_dn = lax.rem(y + 7, 8) * 4 + z
    g_right, g_left = lax.rem(g + 1, 16), lax.rem(g + 15, 16)
    has_lo = jnp.where(y > 0, 1.0, 0.0).astype(f32)
    has_hi = jnp.where(y < 7, 1.0, 0.0).astype(f32)
    has_left = jnp.where(g > 0, 1.0, 0.0).astype(f32)
    has_right = jnp.where(g < 15, 1.0, 0.0).astype(f32)

    def zpeer(dz):
        return lax.rem(z + dz, 4)

    def zfrom(dz):
        return lax.rem(z + 4 - dz, 4)

    def load(i):
        return pltpu.make_async_copy(
            x_hbm.at[0, :, :, pl.ds(ORDER[i] * LANES, LANES)], xbuf.at[i], load_s.at[i]
        )

    def store(i):
        return pltpu.make_async_copy(
            obuf.at[i], o_hbm.at[0, :, :, pl.ds(ORDER[i] * LANES, LANES)], store_s.at[i]
        )

    def remote(src, dst, ss, rs, **to):
        return pltpu.make_async_remote_copy(
            src_ref=src, dst_ref=dst, send_sem=ss, recv_sem=rs, device_id=to, device_id_type=MESH
        )

    def zin(i, dz):
        p = zpeer(dz)
        k = i * 4 + dz
        return remote(sbuf.at[i, p], ebuf.at[i, 4 + z], zin_s.at[k], zin_r.at[k], comp=y * 4 + p)

    def hal_up(i, f):
        k = i * 8 + f
        return remote(ebuf.at[i, 4 + f], ebuf.at[i, f], hal_s.at[k], hal_r.at[k], comp=y_up)

    def hal_dn(i, f):
        k = i * 8 + 4 + f
        return remote(ebuf.at[i, 4 + f], ebuf.at[i, 8 + f], hal_s.at[k], hal_r.at[k], comp=y_dn)

    def bak_dn(i, m):
        k = i * 8 + m
        return remote(tbuf.at[i, m], above.at[i, m], bak_s.at[k], bak_r.at[k], comp=y_dn)

    def bak_up(i, m):
        k = i * 8 + 4 + m
        return remote(tbuf.at[i, 8 + m], below.at[i, m], bak_s.at[k], bak_r.at[k], comp=y_up)

    def zout(i, dz):
        p = zpeer(dz)
        k = i * 4 + dz
        return remote(incr.at[i, p], ibuf.at[i, z], zout_s.at[k], zout_r.at[k], comp=y * 4 + p)

    def lon_to_right():
        return remote(pack_r, halo_l, lon_s.at[0], lon_r.at[0], grid=g_right)

    def lon_to_left():
        return remote(pack_l, halo_r, lon_s.at[1], lon_r.at[1], grid=g_left)

    for i in range(4):
        load(i).start()

    barrier = pltpu.get_barrier_semaphore()
    for dz in (1, 2, 3):
        pl.semaphore_signal(barrier, inc=1, device_id={"comp": y * 4 + zpeer(dz)}, device_id_type=MESH)
    pl.semaphore_signal(barrier, inc=1, device_id={"comp": y_up}, device_id_type=MESH)
    pl.semaphore_signal(barrier, inc=1, device_id={"comp": y_dn}, device_id_type=MESH)
    pl.semaphore_signal(barrier, inc=1, device_id={"grid": g_right}, device_id_type=MESH)
    pl.semaphore_signal(barrier, inc=1, device_id={"grid": g_left}, device_id_type=MESH)

    def lanes(i):
        return slice(ORDER[i] * LANES, (ORDER[i] + 1) * LANES)

    def rows8(rg):
        return pl.ds(pl.multiple_of(rg * 8, 8), 8)

    def prepare(i):
        load(i).wait()
        for dz in (2, 1, 3, 0):
            rg = zpeer(dz)
            sea = mk[rows8(rg), lanes(i)].astype(f32)

            @pl.loop(0, NTH // JB)
            def _(b):
                at = pl.ds(b * JB, JB)
                piece = xbuf[i, at, rows8(rg)] * sea[None]
                sbuf[i, rg, at] = piece
                if dz == 0:
                    ebuf[i, 4 + z, at] = piece

            if i == 0 and dz == 2:
                pl.semaphore_wait(barrier, 7)
            if i == 0 and dz:
                zin(i, dz).start()
        send_halo(i, z)

    wind_w = tab[2, me]
    inv_cel = tab[3, me]
    courant = tab[4, me]

    def grow(i):
        for rg in range(4):
            speed = uw[rg * 8 : rg * 8 + 8, lanes(i)] * inv_cel
            head = wd[rg * 8 : rg * 8 + 8, lanes(i)]
            along, across = speed * jnp.cos(head), speed * jnp.sin(head)

            @pl.loop(0, NTH, unroll=4)
            def _(j):
                growth = wind_w * jnp.maximum(0.0, tab[0, j] * along + tab[1, j] * across - 1.0)
                post[i, rg, j] = sbuf[i, rg, j] * (1.0 + growth)

    def constants():
        row = lax.broadcasted_iota(jnp.int32, (LAT, LANES), 0).astype(f32)

        def cosine(offset):
            return jnp.cos((BAND_CENTRE + (row - offset) * CELL_DEGREES) * (math.pi / 180.0))

        inverse = 1.0 / cosine((LAT - 1) / 2.0)
        rowinv[...] = inverse
        facehi[...] = cosine(LAT / 2.0 - 1.0) * inverse
        facelo[...] = cosine(LAT / 2.0) * inverse
        for i in range(4):
            below[i, 3] = jnp.zeros((NTH, 8, LANES), f32)

    def send_halo(i, f):
        hal_up(i, f).start()

        @pl.when(f < 3)
        def _():
            hal_dn(i, f).start()

    def forward(i):
        for dz in (1, 2, 3):
            zin(i, dz).wait_recv()
            if i < 3:
                zin(i + 1, dz).start()
            send_halo(i, zfrom(dz))

    def interact(i):
        for f in range(4):
            hal_up(i, f).wait_recv()
        for f in range(3):
            hal_dn(i, f).wait_recv()

        @pl.loop(0, 4)
        def _(k):
            lo_a = jnp.where(k < 4, has_lo, 1.0) * D1W
            lo_b = jnp.where(k < 3, has_lo, 1.0) * D0W
            hi_a = jnp.where(k >= 2, has_hi, 1.0) * U0
            hi_b = jnp.where(k >= 1, has_hi, 1.0) * U1

            @pl.loop(0, NTH // JB)
            def _(b):
                at = pl.ds(b * JB, JB)
                to = pl.ds(b * JB + PAD, JB)
                eux[to] = hi_a * ebuf[i, k + 6, at] + hi_b * ebuf[i, k + 7, at]
                edx[to] = lo_b * ebuf[i, k + 1, at] + lo_a * ebuf[i, k, at]

            for ref in (eux, edx):
                ref[0:PAD] = ref[NTH : NTH + PAD]
                ref[NTH + PAD : NTH + 2 * PAD] = ref[PAD : 2 * PAD]

            @pl.loop(0, NTH // JB)
            def _(b):
                def eu(o):
                    return eux[pl.ds(b * JB + PAD + o, JB)]

                def ed(o):
                    return edx[pl.ds(b * JB + PAD + o, JB)]

                e = ebuf[i, k + 4, pl.ds(b * JB, JB)]

                def delta(plus, minus):
                    return e * (e * (W_UP * plus + W_DOWN * minus) - W_CROSS * plus * minus)

                to = pl.ds(b * JB + PAD, JB)
                d1x[to] = delta(N0 * eu(1) + N1 * eu(2), F0 * ed(-3) + F1 * ed(-4))
                d2x[to] = delta(N0 * eu(-1) + N1 * eu(-2), F0 * ed(3) + F1 * ed(4))

            for ref in (d1x, d2x):
                ref[0:PAD] = ref[NTH : NTH + PAD]
                ref[NTH + PAD : NTH + 2 * PAD] = ref[PAD : 2 * PAD]

            @pl.loop(0, NTH // JB)
            def _(b):
                def a1(o):
                    return d1x[pl.ds(b * JB + PAD + o, JB)]

                def a2(o):
                    return d2x[pl.ds(b * JB + PAD + o, JB)]

                at = pl.ds(b * JB, JB)
                bus[k, at] = N0 * (a1(-1) + a2(1)) + N1 * (a1(-2) + a2(2))
                bds[k, at] = F0 * (a1(3) + a2(-3)) + F1 * (a1(4) + a2(-4))
                cen[k, at] = -2.0 * (a1(0) + a2(0))

        @pl.loop(0, NTH)
        def _(j):
            bd = [bds[k, j] for k in range(4)]
            bu = [bus[k, j] for k in range(4)]
            tbuf[i, 0, j] = D1W * bd[0]
            tbuf[i, 1, j] = D0W * bd[0] + D1W * bd[1]
            tbuf[i, 2, j] = D0W * bd[1] + D1W * bd[2]
            tbuf[i, 3, j] = D0W * bd[2] + D1W * bd[3]
            tbuf[i, 4, j] = cen[0, j] + D0W * bd[3]
            tbuf[i, 5, j] = cen[1, j]
            tbuf[i, 6, j] = cen[2, j] + U0 * bu[0]
            tbuf[i, 7, j] = cen[3, j] + U1 * bu[0] + U0 * bu[1]
            tbuf[i, 8, j] = U1 * bu[1] + U0 * bu[2]
            tbuf[i, 9, j] = U1 * bu[2] + U0 * bu[3]
            tbuf[i, 10, j] = U1 * bu[3]

        for m in range(4):
            bak_dn(i, m).start()
            if m < 3:
                bak_up(i, m).start()

    def gather(i):
        for dz in (1, 2, 3, 0):
            m = zpeer(dz)
            bak_dn(i, m).wait_recv()

            @pl.when(m < 3)
            def _():
                bak_up(i, m).wait_recv()

            total = tbuf[i, 4 + m] + has_hi * above[i, m] + has_lo * below[i, m]
            if dz == 0:
                ibuf[i, z] = total
            else:
                incr[i, m] = total
                zout(i, dz).start()

    def finish(i):
        for dz in (1, 2, 3):
            zout(i, dz).wait_recv()

        @pl.loop(0, NTH // JB)
        def _(b):
            at = pl.ds(b * JB, JB)
            for rg in range(4):
                post[i, rg, at] = post[i, rg, at] + ibuf[i, rg, at]

    lane = lax.broadcasted_iota(jnp.int32, (8, LANES), 1)

    def edges():
        first, last = ORDER.index(0), ORDER.index(3)
        for rg in range(4):

            def step(j, acc):
                a, b = acc
                here = (lane == 2 * j) | (lane == 2 * j + 1)
                a = jnp.where(here, pltpu.roll(post[first, rg, j], 2 * j, 1), a)
                b = jnp.where(here, pltpu.roll(post[last, rg, j], 2 * j + 2, 1), b)
                return a, b

            zero = jnp.zeros((8, LANES), f32)
            a, b = lax.fori_loop(0, NTH, step, (zero, zero), unroll=4)
            pack_l[rg] = a
            pack_r[rg] = b
        lon_to_right().start()
        lon_to_left().start()

    sub = lax.broadcasted_iota(jnp.int32, (8, LANES), 0)

    def shift(here, other, by, axis):
        size = LANES if axis else 8
        place = lane if axis else sub
        if by > 0:
            return pltpu.roll(jnp.where(place >= size - by, other, here), by, axis)
        return pltpu.roll(jnp.where(place < -by, other, here), size + by, axis)

    def sweep_x(c, v, left, right, positive):
        c = c if positive else -c
        q = (1.0 - c * c) * (1.0 / 6.0)
        mid = 0.5 + 0.5 * c + 2.0 * q
        far = 0.5 - 0.5 * c - q
        k_next, k_here = c * far, 1.0 - c * (mid - far)
        k_back, k_back2 = c * (q + mid), c * q
        outs = []
        for here, low, high in zip(v, left, right, strict=True):
            up, dn = (low, high) if positive else (high, low)
            way = 1 if positive else -1
            nxt = shift(here, dn, -way, 1)
            back = shift(here, up, way, 1)
            back2 = shift(here, up, 2 * way, 1)
            outs.append(k_here * here - k_next * nxt + k_back * back - k_back2 * back2)
        return outs

    def sweep_y(c, u, positive):
        q = (1.0 - c * c) * (1.0 / 6.0)
        zero = jnp.zeros((8, LANES), f32)
        tiles = [zero, *u, zero]
        faces = []
        if positive:
            t_back, t_here, t_next = -q * c, c * (0.5 + 0.5 * c + 2.0 * q), c * (0.5 - 0.5 * c - q)
        else:
            t_here, t_next, t_next2 = c * (0.5 + 0.5 * c - q), c * (0.5 - 0.5 * c + 2.0 * q), -q * c
        for r in range(5):
            here = tiles[r]
            high = tiles[r + 1]
            face = t_here * here + t_next * shift(here, high, -1, 0)
            if positive:
                if r:
                    face = face + t_back * shift(here, tiles[r - 1], 1, 0)
            else:
                face = face + t_next2 * shift(here, high, -2, 0)
            faces.append(face)
        outs = []
        for r in range(4):
            over, under = faces[r + 1], shift(faces[r + 1], faces[r], 1, 0)
            at = slice(r * 8, r * 8 + 8)
            outs.append(u[r] - (facehi[at] * over - facelo[at] * under))
        return outs

    def propagate(chunks):
        @pl.loop(0, NTH // 4)
        def _(t):
            for quarter in range(4):
                j = t + 9 * quarter
                x_pos, y_pos = quarter in (0, 3), quarter in (0, 1)
                swept = [[None] * 4 for _ in chunks]
                for rg in range(4):
                    v = {col: post[ORDER.index(col), rg, j] for col in range(4)}
                    if 0 in chunks:
                        v[-1] = has_left * pltpu.roll(halo_l[rg], 126 - 2 * j, 1)
                    if 3 in chunks:
                        v[4] = has_right * pltpu.roll(halo_r[rg], LANES - 2 * j, 1)
                    outs = sweep_x(
                        (courant * tab[0, j]) * rowinv[rg * 8 : rg * 8 + 8],
                        [v[col] for col in chunks],
                        [v[col - 1] for col in chunks],
                        [v[col + 1] for col in chunks],
                        x_pos,
                    )
                    for n, out in enumerate(outs):
                        sea = mk[rg * 8 : rg * 8 + 8, lanes(ORDER.index(chunks[n]))]
                        swept[n][rg] = out * sea.astype(f32)
                for n, col in enumerate(chunks):
                    outs = sweep_y(courant * tab[1, j], swept[n], y_pos)
                    for rg in range(4):
                        at = slice(rg * 8, rg * 8 + 8)
                        sea = mk[at, lanes(ORDER.index(col))].astype(f32)
                        obuf[ORDER.index(col), j, at] = outs[rg] * sea

        for col in chunks:
            store(ORDER.index(col)).start()

    for i in range(4):
        prepare(i)
    constants()
    grow(0)
    forward(0)
    grow(1)
    forward(1)
    interact(0)
    grow(2)
    forward(2)
    interact(1)
    grow(3)
    gather(0)
    forward(3)
    interact(2)
    gather(1)
    interact(3)
    finish(0)
    gather(2)
    finish(1)
    edges()
    gather(3)
    finish(2)
    lon_to_right().wait_recv()
    lon_to_left().wait_recv()
    propagate((0,))
    finish(3)
    propagate((1, 2, 3))

    for i in range(4):
        for dz in (1, 2, 3):
            zin(i, dz).wait_send()
            zout(i, dz).wait_send()
        for f in range(4):
            hal_up(i, f).wait_send()
            bak_dn(i, f).wait_send()
        for f in range(3):
            hal_dn(i, f).wait_send()
            bak_up(i, f).wait_send()
        store(i).wait()
    lon_to_right().wait_send()
    lon_to_left().wait_send()


def shards(spectra, u_wind, wind_dir, sea_mask):
    f32 = jnp.float32
    tile = (NTH, 8, LANES)
    vmem, dma = pltpu.VMEM, pltpu.SemaphoreType.DMA
    inner = pl.BlockSpec(memory_space=pltpu.VMEM)
    columns = jnp.transpose(spectra, (0, 2, 1, 3))
    result = pl.pallas_call(
        kernel,
        out_shape=jax.ShapeDtypeStruct(columns.shape, f32),
        in_specs=[
            pl.BlockSpec(memory_space=pltpu.SMEM),
            pl.BlockSpec(memory_space=pl.ANY),
            inner, inner, inner,
        ],
        out_specs=pl.BlockSpec(memory_space=pl.ANY),
        scratch_shapes=[
            vmem((4, NTH, LAT, LANES), f32),
            vmem((4, NTH, LAT, LANES), f32),
            vmem((4, 4) + tile, f32),
            vmem((4, 11) + tile, f32),
            vmem((4, 11) + tile, f32),
            vmem((4, 4) + tile, f32),
            vmem((4, 4) + tile, f32),
            vmem((4, 4) + tile, f32),
            vmem((4, 4) + tile, f32),
            vmem((4, 4) + tile, f32),
            vmem((NTH + 2 * PAD, 8, LANES), f32),
            vmem((NTH + 2 * PAD, 8, LANES), f32),
            vmem((NTH + 2 * PAD, 8, LANES), f32),
            vmem((NTH + 2 * PAD, 8, LANES), f32),
            vmem((4,) + tile, f32),
            vmem((4,) + tile, f32),
            vmem((4,) + tile, f32),
            vmem((LAT, LANES), f32),
            vmem((LAT, LANES), f32),
            vmem((LAT, LANES), f32),
            vmem((4, 8, LANES), f32),
            vmem((4, 8, LANES), f32),
            vmem((4, 8, LANES), f32),
            vmem((4, 8, LANES), f32),
            dma((4,)), dma((4,)),
            dma((16,)), dma((16,)),
            dma((32,)), dma((32,)),
            dma((32,)), dma((32,)),
            dma((16,)), dma((16,)),
            dma((2,)), dma((2,)),
        ],
        compiler_params=pltpu.CompilerParams(
            collective_id=0, has_side_effects=True, vmem_limit_bytes=56 << 20
        ),
        cost_estimate=pl.CostEstimate(flops=60_000_000, bytes_accessed=5_000_000, transcendentals=32_768),
        name="wave_step",
    )(tables(), columns, u_wind, wind_dir, sea_mask)
    return jnp.transpose(result, (0, 2, 1, 3))


def solution(mesh):
    return jax.shard_map(
        shards,
        mesh=mesh,
        in_specs=(P("comp", None, None, "grid"), P(None, "grid"), P(None, "grid"), P(None, "grid")),
        out_specs=P("comp", None, None, "grid"),
        check_vma=False,
    )
```

```python
import math

import numpy as np

import jax
import jax.numpy as jnp
from jax import lax
from jax.experimental import pallas as pl
from jax.experimental.pallas import tpu as pltpu
from jax.sharding import PartitionSpec as P

MESH = pl.DeviceIdType.MESH
NK, NTH, LAT = 32, 36, 32
GRAVITY = 9.81
LAMBDA = 0.25
WIND = 0.0003125 * 120.0
ADVECT_STEP = 220.0
EARTH_RADIUS = 6371000.0
BAND_CENTRE = 30.0
CELL_DEGREES = 0.05
CELL_RADIANS = CELL_DEGREES * math.pi / 180.0
SHIFT_UP = math.log(1.0 + LAMBDA) / math.log(1.1)
SHIFT_DOWN = math.log(1.0 - LAMBDA) / math.log(1.1)
NEAR = 11.48 * NTH / 360.0
FAR = 33.56 * NTH / 360.0
U1 = SHIFT_UP - 2.0
U0 = 1.0 - U1
D1W = -SHIFT_DOWN - 3.0
D0W = 1.0 - D1W
N1 = NEAR - 1.0
N0 = 1.0 - N1
F1 = FAR - 3.0
F0 = 1.0 - F1
W_UP = 0.1 / (1.0 + LAMBDA) ** 4
W_DOWN = 0.1 / (1.0 - LAMBDA) ** 4
W_CROSS = 0.2 / (1.0 - LAMBDA * LAMBDA) ** 4

ORDER = (0, 3, 1, 2)
LANES = 128
HALF = NTH // 2
JB = 4
PAD = 4


def tables():
    t = np.zeros((8, 128), np.float64)
    th = 2.0 * np.pi * np.arange(NTH) / NTH
    t[0, :NTH] = np.cos(th)
    t[1, :NTH] = np.sin(th)
    f = 0.04 * 1.1 ** np.arange(NK)
    w = 2.0 * np.pi * f
    t[2, :NK] = WIND * w
    t[3, :NK] = w / GRAVITY
    t[4, :NK] = GRAVITY / (2.0 * w) * ADVECT_STEP / (EARTH_RADIUS * CELL_RADIANS)
    return t.astype(np.float32)


def kernel(
    tab, x_hbm, uw, wd, mk, o_hbm,
    xbuf, obuf, sbuf, ebuf, tbuf, above, below, incr, ibuf, post,
    eux, edx, d1x, d2x, bus, bds, cen, rowinv, facehi, facelo,
    pack_l, pack_r, halo_l, halo_r,
    load_s, store_s, zin_s, zin_r, hal_s, hal_r, bak_s, bak_r, zout_s, zout_r, lon_s, lon_r,
):
    f32 = jnp.float32
    me = lax.axis_index("comp")
    g = lax.axis_index("grid")
    y, z = me // 4, lax.rem(me, 4)
    y_up = lax.rem(y + 1, 8) * 4 + z
    y_dn = lax.rem(y + 7, 8) * 4 + z
    g_right, g_left = lax.rem(g + 1, 16), lax.rem(g + 15, 16)
    has_lo = jnp.where(y > 0, 1.0, 0.0).astype(f32)
    has_hi = jnp.where(y < 7, 1.0, 0.0).astype(f32)
    has_left = jnp.where(g > 0, 1.0, 0.0).astype(f32)
    has_right = jnp.where(g < 15, 1.0, 0.0).astype(f32)

    def zpeer(dz):
        return lax.rem(z + dz, 4)

    def zfrom(dz):
        return lax.rem(z + 4 - dz, 4)

    def load(i):
        return pltpu.make_async_copy(
            x_hbm.at[0, :, :, pl.ds(ORDER[i] * LANES, LANES)], xbuf.at[i], load_s.at[i]
        )

    def store(i, half):
        at = pl.ds(half * HALF, HALF)
        return pltpu.make_async_copy(
            obuf.at[i, at], o_hbm.at[0, at, :, pl.ds(ORDER[i] * LANES, LANES)], store_s.at[i * 2 + half]
        )

    def part(i, half):
        return pl.ds(half * HALF, HALF) if i == 3 else pl.ds(0, NTH)

    def remote(src, dst, ss, rs, **to):
        return pltpu.make_async_remote_copy(
            src_ref=src, dst_ref=dst, send_sem=ss, recv_sem=rs, device_id=to, device_id_type=MESH
        )

    def zin(i, dz):
        p = zpeer(dz)
        k = i * 4 + dz
        return remote(sbuf.at[i, p], ebuf.at[i, 4 + z], zin_s.at[k], zin_r.at[k], comp=y * 4 + p)

    def hal_up(i, f):
        k = i * 8 + f
        return remote(ebuf.at[i, 4 + f], ebuf.at[i, f], hal_s.at[k], hal_r.at[k], comp=y_up)

    def hal_dn(i, f):
        k = i * 8 + 4 + f
        return remote(ebuf.at[i, 4 + f], ebuf.at[i, 8 + f], hal_s.at[k], hal_r.at[k], comp=y_dn)

    def bak_dn(i, m, half=0):
        k, at = (i + half) * 8 + m, part(i, half)
        return remote(tbuf.at[i, m, at], above.at[i, m, at], bak_s.at[k], bak_r.at[k], comp=y_dn)

    def bak_up(i, m, half=0):
        k, at = (i + half) * 8 + 4 + m, part(i, half)
        return remote(tbuf.at[i, 8 + m, at], below.at[i, m, at], bak_s.at[k], bak_r.at[k], comp=y_up)

    def zout(i, dz, half=0):
        p, at = zpeer(dz), part(i, half)
        k = (i + half) * 4 + dz
        return remote(incr.at[i, p, at], ibuf.at[i, z, at], zout_s.at[k], zout_r.at[k], comp=y * 4 + p)

    def lon_to_right():
        return remote(pack_r, halo_l, lon_s.at[0], lon_r.at[0], grid=g_right)

    def lon_to_left():
        return remote(pack_l, halo_r, lon_s.at[1], lon_r.at[1], grid=g_left)

    for i in range(4):
        load(i).start()

    barrier = pltpu.get_barrier_semaphore()
    for dz in (1, 2, 3):
        pl.semaphore_signal(barrier, inc=1, device_id={"comp": y * 4 + zpeer(dz)}, device_id_type=MESH)
    pl.semaphore_signal(barrier, inc=1, device_id={"comp": y_up}, device_id_type=MESH)
    pl.semaphore_signal(barrier, inc=1, device_id={"comp": y_dn}, device_id_type=MESH)
    pl.semaphore_signal(barrier, inc=1, device_id={"grid": g_right}, device_id_type=MESH)
    pl.semaphore_signal(barrier, inc=1, device_id={"grid": g_left}, device_id_type=MESH)

    def lanes(i):
        return slice(ORDER[i] * LANES, (ORDER[i] + 1) * LANES)

    def rows8(rg):
        return pl.ds(pl.multiple_of(rg * 8, 8), 8)

    def prepare(i):
        load(i).wait()
        for dz in (2, 1, 3, 0):
            rg = zpeer(dz)
            sea = mk[rows8(rg), lanes(i)].astype(f32)

            @pl.loop(0, NTH // JB)
            def _(b):
                at = pl.ds(b * JB, JB)
                piece = xbuf[i, at, rows8(rg)] * sea[None]
                sbuf[i, rg, at] = piece
                if dz == 0:
                    ebuf[i, 4 + z, at] = piece

            if i == 0 and dz == 2:
                pl.semaphore_wait(barrier, 7)
            if i == 0 and dz:
                zin(i, dz).start()
        send_halo(i, z)

    wind_w = tab[2, me]
    inv_cel = tab[3, me]
    courant = tab[4, me]

    def grow(i):
        for rg in range(4):
            speed = uw[rg * 8 : rg * 8 + 8, lanes(i)] * inv_cel
            head = wd[rg * 8 : rg * 8 + 8, lanes(i)]
            along, across = speed * jnp.cos(head), speed * jnp.sin(head)

            @pl.loop(0, NTH, unroll=4)
            def _(j):
                growth = wind_w * jnp.maximum(0.0, tab[0, j] * along + tab[1, j] * across - 1.0)
                post[i, rg, j] = sbuf[i, rg, j] * (1.0 + growth)

    def constants():
        row = lax.broadcasted_iota(jnp.int32, (LAT, LANES), 0).astype(f32)

        def cosine(offset):
            return jnp.cos((BAND_CENTRE + (row - offset) * CELL_DEGREES) * (math.pi / 180.0))

        inverse = 1.0 / cosine((LAT - 1) / 2.0)
        rowinv[...] = inverse
        facehi[...] = cosine(LAT / 2.0 - 1.0) * inverse
        facelo[...] = cosine(LAT / 2.0) * inverse
        for i in range(4):
            below[i, 3] = jnp.zeros((NTH, 8, LANES), f32)

    def send_halo(i, f):
        hal_up(i, f).start()

        @pl.when(f < 3)
        def _():
            hal_dn(i, f).start()

    def forward(i):
        for dz in (1, 2, 3):
            zin(i, dz).wait_recv()
            if i < 3:
                zin(i + 1, dz).start()
            send_halo(i, zfrom(dz))

    def interact(i):
        for f in range(4):
            hal_up(i, f).wait_recv()
        for f in range(3):
            hal_dn(i, f).wait_recv()

        @pl.loop(0, 4)
        def _(k):
            lo_a = jnp.where(k < 4, has_lo, 1.0) * D1W
            lo_b = jnp.where(k < 3, has_lo, 1.0) * D0W
            hi_a = jnp.where(k >= 2, has_hi, 1.0) * U0
            hi_b = jnp.where(k >= 1, has_hi, 1.0) * U1

            @pl.loop(0, NTH // JB)
            def _(b):
                at = pl.ds(b * JB, JB)
                to = pl.ds(b * JB + PAD, JB)
                eux[to] = hi_a * ebuf[i, k + 6, at] + hi_b * ebuf[i, k + 7, at]
                edx[to] = lo_b * ebuf[i, k + 1, at] + lo_a * ebuf[i, k, at]

            for ref in (eux, edx):
                ref[0:PAD] = ref[NTH : NTH + PAD]
                ref[NTH + PAD : NTH + 2 * PAD] = ref[PAD : 2 * PAD]

            @pl.loop(0, NTH // JB)
            def _(b):
                def eu(o):
                    return eux[pl.ds(b * JB + PAD + o, JB)]

                def ed(o):
                    return edx[pl.ds(b * JB + PAD + o, JB)]

                e = ebuf[i, k + 4, pl.ds(b * JB, JB)]

                def delta(plus, minus):
                    return e * (e * (W_UP * plus + W_DOWN * minus) - W_CROSS * plus * minus)

                to = pl.ds(b * JB + PAD, JB)
                d1x[to] = delta(N0 * eu(1) + N1 * eu(2), F0 * ed(-3) + F1 * ed(-4))
                d2x[to] = delta(N0 * eu(-1) + N1 * eu(-2), F0 * ed(3) + F1 * ed(4))

            for ref in (d1x, d2x):
                ref[0:PAD] = ref[NTH : NTH + PAD]
                ref[NTH + PAD : NTH + 2 * PAD] = ref[PAD : 2 * PAD]

            @pl.loop(0, NTH // JB)
            def _(b):
                def a1(o):
                    return d1x[pl.ds(b * JB + PAD + o, JB)]

                def a2(o):
                    return d2x[pl.ds(b * JB + PAD + o, JB)]

                at = pl.ds(b * JB, JB)
                bus[k, at] = N0 * (a1(-1) + a2(1)) + N1 * (a1(-2) + a2(2))
                bds[k, at] = F0 * (a1(3) + a2(-3)) + F1 * (a1(4) + a2(-4))
                cen[k, at] = -2.0 * (a1(0) + a2(0))

        @pl.loop(0, NTH)
        def _(j):
            bd = [bds[k, j] for k in range(4)]
            bu = [bus[k, j] for k in range(4)]
            tbuf[i, 0, j] = D1W * bd[0]
            tbuf[i, 1, j] = D0W * bd[0] + D1W * bd[1]
            tbuf[i, 2, j] = D0W * bd[1] + D1W * bd[2]
            tbuf[i, 3, j] = D0W * bd[2] + D1W * bd[3]
            tbuf[i, 4, j] = cen[0, j] + D0W * bd[3]
            tbuf[i, 5, j] = cen[1, j]
            tbuf[i, 6, j] = cen[2, j] + U0 * bu[0]
            tbuf[i, 7, j] = cen[3, j] + U1 * bu[0] + U0 * bu[1]
            tbuf[i, 8, j] = U1 * bu[1] + U0 * bu[2]
            tbuf[i, 9, j] = U1 * bu[2] + U0 * bu[3]
            tbuf[i, 10, j] = U1 * bu[3]

        for dz in (1, 2, 3, 0):
            m = zpeer(dz)
            bak_dn(i, m).start()

            @pl.when(m < 3)
            def _():
                bak_up(i, m).start()

    def gather(i, half=0):
        at = part(i, half)
        for dz in (1, 2, 3, 0):
            m = zpeer(dz)
            more = i == 3 and half == 0
            bak_dn(i, m, half).wait_recv()
            if more:
                bak_dn(i, m, 1).start()

            @pl.when(m < 3)
            def _():
                bak_up(i, m, half).wait_recv()
                if more:
                    bak_up(i, m, 1).start()

            total = tbuf[i, 4 + m, at] + has_hi * above[i, m, at] + has_lo * below[i, m, at]
            if dz == 0:
                ibuf[i, z, at] = total
            else:
                incr[i, m, at] = total
                zout(i, dz, half).start()

    def finish(i, half=0):
        for dz in (1, 2, 3):
            zout(i, dz, half).wait_recv()
        whole = part(i, half).size

        @pl.loop(0, whole // 6)
        def _(b):
            at = pl.ds(half * HALF + b * 6, 6)
            for rg in range(4):
                post[i, rg, at] = post[i, rg, at] + ibuf[i, rg, at]

    lane = lax.broadcasted_iota(jnp.int32, (8, LANES), 1)

    def edges():
        first, last = ORDER.index(0), ORDER.index(3)

        @pl.loop(0, 4)
        def _(rg):
            a, b = post[first, rg, 0], pltpu.roll(post[last, rg, 0], 2, 1)
            for j in range(1, NTH):
                here = lane >= 2 * j
                a = jnp.where(here, pltpu.roll(post[first, rg, j], 2 * j, 1), a)
                b = jnp.where(here, pltpu.roll(post[last, rg, j], 2 * j + 2, 1), b)
            pack_l[rg] = a
            pack_r[rg] = b

        lon_to_right().start()
        lon_to_left().start()

    sub = lax.broadcasted_iota(jnp.int32, (8, LANES), 0)

    def shift(here, other, by, axis):
        size = LANES if axis else 8
        place = lane if axis else sub
        if by > 0:
            return pltpu.roll(jnp.where(place >= size - by, other, here), by, axis)
        return pltpu.roll(jnp.where(place < -by, other, here), size + by, axis)

    def sweep_x(c, v, left, right, positive):
        c = c if positive else -c
        q = (1.0 - c * c) * (1.0 / 6.0)
        mid = 0.5 + 0.5 * c + 2.0 * q
        far = 0.5 - 0.5 * c - q
        k_next, k_here = c * far, 1.0 - c * (mid - far)
        k_back, k_back2 = c * (q + mid), c * q
        outs = []
        for here, low, high in zip(v, left, right, strict=True):
            up, dn = (low, high) if positive else (high, low)
            way = 1 if positive else -1
            nxt = shift(here, dn, -way, 1)
            back = shift(here, up, way, 1)
            back2 = shift(here, up, 2 * way, 1)
            outs.append(k_here * here - k_next * nxt + k_back * back - k_back2 * back2)
        return outs

    def sweep_y(c, u, positive):
        q = (1.0 - c * c) * (1.0 / 6.0)
        zero = jnp.zeros((8, LANES), f32)
        tiles = [zero, *u, zero]
        faces = []
        if positive:
            t_back, t_here, t_next = -q * c, c * (0.5 + 0.5 * c + 2.0 * q), c * (0.5 - 0.5 * c - q)
        else:
            t_here, t_next, t_next2 = c * (0.5 + 0.5 * c - q), c * (0.5 - 0.5 * c + 2.0 * q), -q * c
        for r in range(5):
            here = tiles[r]
            high = tiles[r + 1]
            face = t_here * here + t_next * shift(here, high, -1, 0)
            if positive:
                if r:
                    face = face + t_back * shift(here, tiles[r - 1], 1, 0)
            else:
                face = face + t_next2 * shift(here, high, -2, 0)
            faces.append(face)
        outs = []
        for r in range(4):
            over, under = faces[r + 1], shift(faces[r + 1], faces[r], 1, 0)
            at = slice(r * 8, r * 8 + 8)
            outs.append(u[r] - (facehi[at] * over - facelo[at] * under))
        return outs

    def propagate(chunks, half):
        @pl.loop(0, NTH // 4)
        def _(t):
            for quarter in (2 * half, 2 * half + 1):
                j = t + 9 * quarter
                x_pos, y_pos = quarter in (0, 3), quarter in (0, 1)
                swept = [[None] * 4 for _ in chunks]
                for rg in range(4):
                    v = {col: post[ORDER.index(col), rg, j] for col in range(4)}
                    if 0 in chunks:
                        v[-1] = has_left * pltpu.roll(halo_l[rg], 126 - 2 * j, 1)
                    if 3 in chunks:
                        v[4] = has_right * pltpu.roll(halo_r[rg], LANES - 2 * j, 1)
                    outs = sweep_x(
                        (courant * tab[0, j]) * rowinv[rg * 8 : rg * 8 + 8],
                        [v[col] for col in chunks],
                        [v[col - 1] for col in chunks],
                        [v[col + 1] for col in chunks],
                        x_pos,
                    )
                    for n, out in enumerate(outs):
                        sea = mk[rg * 8 : rg * 8 + 8, lanes(ORDER.index(chunks[n]))]
                        swept[n][rg] = out * sea.astype(f32)
                for n, col in enumerate(chunks):
                    outs = sweep_y(courant * tab[1, j], swept[n], y_pos)
                    for rg in range(4):
                        at = slice(rg * 8, rg * 8 + 8)
                        sea = mk[at, lanes(ORDER.index(col))].astype(f32)
                        obuf[ORDER.index(col), j, at] = outs[rg] * sea

        for col in chunks:
            store(ORDER.index(col), half).start()

    for i in range(4):
        prepare(i)
    constants()
    grow(0)
    forward(0)
    grow(1)
    forward(1)
    interact(0)
    grow(2)
    forward(2)
    interact(1)
    grow(3)
    gather(0)
    forward(3)
    interact(2)
    gather(1)
    interact(3)
    finish(0)
    gather(2)
    finish(1)
    edges()
    gather(3, 0)
    gather(3, 1)
    finish(2)
    lon_to_right().wait_recv()
    lon_to_left().wait_recv()
    propagate((0,), 0)
    propagate((0,), 1)
    finish(3, 0)
    propagate((1, 2, 3), 0)
    finish(3, 1)
    propagate((1, 2, 3), 1)

    for i in range(4):
        for dz in (1, 2, 3):
            zin(i, dz).wait_send()
        for f in range(4):
            hal_up(i, f).wait_send()
        for f in range(3):
            hal_dn(i, f).wait_send()
        for half in range(2 if i == 3 else 1):
            for dz in (1, 2, 3):
                zout(i, dz, half).wait_send()
            for m in range(4):
                bak_dn(i, m, half).wait_send()
            for m in range(3):
                bak_up(i, m, half).wait_send()
        store(i, 0).wait()
        store(i, 1).wait()
    lon_to_right().wait_send()
    lon_to_left().wait_send()


def shards(spectra, u_wind, wind_dir, sea_mask):
    f32 = jnp.float32
    tile = (NTH, 8, LANES)
    vmem, dma = pltpu.VMEM, pltpu.SemaphoreType.DMA
    inner = pl.BlockSpec(memory_space=pltpu.VMEM)
    columns = jnp.transpose(spectra, (0, 2, 1, 3))
    result = pl.pallas_call(
        kernel,
        out_shape=jax.ShapeDtypeStruct(columns.shape, f32),
        in_specs=[
            pl.BlockSpec(memory_space=pltpu.SMEM),
            pl.BlockSpec(memory_space=pl.ANY),
            inner, inner, inner,
        ],
        out_specs=pl.BlockSpec(memory_space=pl.ANY),
        scratch_shapes=[
            vmem((4, NTH, LAT, LANES), f32),
            vmem((4, NTH, LAT, LANES), f32),
            vmem((4, 4) + tile, f32),
            vmem((4, 11) + tile, f32),
            vmem((4, 11) + tile, f32),
            vmem((4, 4) + tile, f32),
            vmem((4, 4) + tile, f32),
            vmem((4, 4) + tile, f32),
            vmem((4, 4) + tile, f32),
            vmem((4, 4) + tile, f32),
            vmem((NTH + 2 * PAD, 8, LANES), f32),
            vmem((NTH + 2 * PAD, 8, LANES), f32),
            vmem((NTH + 2 * PAD, 8, LANES), f32),
            vmem((NTH + 2 * PAD, 8, LANES), f32),
            vmem((4,) + tile, f32),
            vmem((4,) + tile, f32),
            vmem((4,) + tile, f32),
            vmem((LAT, LANES), f32),
            vmem((LAT, LANES), f32),
            vmem((LAT, LANES), f32),
            vmem((4, 8, LANES), f32),
            vmem((4, 8, LANES), f32),
            vmem((4, 8, LANES), f32),
            vmem((4, 8, LANES), f32),
            dma((4,)), dma((8,)),
            dma((16,)), dma((16,)),
            dma((32,)), dma((32,)),
            dma((40,)), dma((40,)),
            dma((20,)), dma((20,)),
            dma((2,)), dma((2,)),
        ],
        compiler_params=pltpu.CompilerParams(
            collective_id=0, has_side_effects=True, vmem_limit_bytes=56 << 20
        ),
        cost_estimate=pl.CostEstimate(flops=60_000_000, bytes_accessed=5_000_000, transcendentals=32_768),
        name="wave_step",
    )(tables(), columns, u_wind, wind_dir, sea_mask)
    return jnp.transpose(result, (0, 2, 1, 3))


def solution(mesh):
    return jax.shard_map(
        shards,
        mesh=mesh,
        in_specs=(P("comp", None, None, "grid"), P(None, "grid"), P(None, "grid"), P(None, "grid")),
        out_specs=P("comp", None, None, "grid"),
        check_vma=False,
    )
```

```python
import math

import numpy as np

import jax
import jax.numpy as jnp
from jax import lax
from jax.experimental import pallas as pl
from jax.experimental.pallas import tpu as pltpu
from jax.sharding import PartitionSpec as P

MESH = pl.DeviceIdType.MESH
NK, NTH, LAT = 32, 36, 32
GRAVITY = 9.81
LAMBDA = 0.25
WIND = 0.0003125 * 120.0
ADVECT_STEP = 220.0
EARTH_RADIUS = 6371000.0
BAND_CENTRE = 30.0
CELL_DEGREES = 0.05
CELL_RADIANS = CELL_DEGREES * math.pi / 180.0
SHIFT_UP = math.log(1.0 + LAMBDA) / math.log(1.1)
SHIFT_DOWN = math.log(1.0 - LAMBDA) / math.log(1.1)
NEAR = 11.48 * NTH / 360.0
FAR = 33.56 * NTH / 360.0
U1 = SHIFT_UP - 2.0
U0 = 1.0 - U1
D1W = -SHIFT_DOWN - 3.0
D0W = 1.0 - D1W
N1 = NEAR - 1.0
N0 = 1.0 - N1
F1 = FAR - 3.0
F0 = 1.0 - F1
W_UP = 0.1 / (1.0 + LAMBDA) ** 4
W_DOWN = 0.1 / (1.0 - LAMBDA) ** 4
W_CROSS = 0.2 / (1.0 - LAMBDA * LAMBDA) ** 4

ORDER = (0, 3, 1, 2)
WINDOW = (0, 1, 0, 1)
LANES = 128
HALF = NTH // 2
JB = 4
PAD = 4


def tables():
    t = np.zeros((8, 128), np.float64)
    th = 2.0 * np.pi * np.arange(NTH) / NTH
    t[0, :NTH] = np.cos(th)
    t[1, :NTH] = np.sin(th)
    f = 0.04 * 1.1 ** np.arange(NK)
    w = 2.0 * np.pi * f
    t[2, :NK] = WIND * w
    t[3, :NK] = w / GRAVITY
    t[4, :NK] = GRAVITY / (2.0 * w) * ADVECT_STEP / (EARTH_RADIUS * CELL_RADIANS)
    return t.astype(np.float32)


def halo_ups(i):
    return range(1, 4) if WINDOW[i] else range(4)


def halo_dns(i):
    return range(4) if WINDOW[i] else range(3)


def back_ups(i):
    return range(4) if WINDOW[i] else range(3)


def back_dns(i):
    return range(1, 4) if WINDOW[i] else range(4)


def kernel(
    tab, x_hbm, uw, wd, mk, o_hbm,
    xbuf, obuf, sbuf, ebuf, tbuf, above, below, incr, ibuf, post,
    eux, edx, d1x, d2x, bus, bds, cen, rowinv, facehi, facelo,
    pack_l, pack_r, halo_l, halo_r,
    load_s, store_s, zin_s, zin_r, hal_s, hal_r, bak_s, bak_r, zout_s, zout_r, lon_s, lon_r,
):
    f32 = jnp.float32
    me = lax.axis_index("comp")
    g = lax.axis_index("grid")
    y, z = me // 4, lax.rem(me, 4)
    y_up = lax.rem(y + 1, 8) * 4 + z
    y_dn = lax.rem(y + 7, 8) * 4 + z
    g_right, g_left = lax.rem(g + 1, 16), lax.rem(g + 15, 16)
    has_lo = jnp.where(y > 0, 1.0, 0.0).astype(f32)
    has_hi = jnp.where(y < 7, 1.0, 0.0).astype(f32)
    has_left = jnp.where(g > 0, 1.0, 0.0).astype(f32)
    has_right = jnp.where(g < 15, 1.0, 0.0).astype(f32)

    def zpeer(dz):
        return lax.rem(z + dz, 4)

    def zfrom(dz):
        return lax.rem(z + 4 - dz, 4)

    def load(i):
        return pltpu.make_async_copy(
            x_hbm.at[0, :, :, pl.ds(ORDER[i] * LANES, LANES)], xbuf.at[i], load_s.at[i]
        )

    def store(i, half):
        at = pl.ds(half * HALF, HALF)
        return pltpu.make_async_copy(
            obuf.at[i, at], o_hbm.at[0, at, :, pl.ds(ORDER[i] * LANES, LANES)], store_s.at[i * 2 + half]
        )

    def travels(i, f, four, action):
        if four:
            action()
        else:

            @pl.when(f >= 1 if WINDOW[i] else f < 3)
            def _():
                action()

    def halo_each(i, f, up, down):
        travels(i, f, WINDOW[i] == 0, up)
        travels(i, f, WINDOW[i] == 1, down)

    def back_each(i, m, up, down):
        travels(i, m, WINDOW[i] == 1, up)
        travels(i, m, WINDOW[i] == 0, down)

    def part(i, half):
        return pl.ds(half * HALF, HALF) if i == 3 else pl.ds(0, NTH)

    def remote(src, dst, ss, rs, **to):
        return pltpu.make_async_remote_copy(
            src_ref=src, dst_ref=dst, send_sem=ss, recv_sem=rs, device_id=to, device_id_type=MESH
        )

    def zin(i, dz):
        p = zpeer(dz)
        k = i * 4 + dz
        return remote(sbuf.at[i, p], ebuf.at[i, 4 + z], zin_s.at[k], zin_r.at[k], comp=y * 4 + p)

    def hal_up(i, f):
        k = i * 8 + f
        return remote(ebuf.at[i, 4 + f], ebuf.at[i, f], hal_s.at[k], hal_r.at[k], comp=y_up)

    def hal_dn(i, f):
        k = i * 8 + 4 + f
        return remote(ebuf.at[i, 4 + f], ebuf.at[i, 8 + f], hal_s.at[k], hal_r.at[k], comp=y_dn)

    def bak_dn(i, m, half=0):
        k, at = (i + half) * 8 + m, part(i, half)
        return remote(tbuf.at[i, m, at], above.at[i, m, at], bak_s.at[k], bak_r.at[k], comp=y_dn)

    def bak_up(i, m, half=0):
        k, at = (i + half) * 8 + 4 + m, part(i, half)
        return remote(tbuf.at[i, 8 + m, at], below.at[i, m, at], bak_s.at[k], bak_r.at[k], comp=y_up)

    def zout(i, dz, half=0):
        p, at = zpeer(dz), part(i, half)
        k = (i + half) * 4 + dz
        return remote(incr.at[i, p, at], ibuf.at[i, z, at], zout_s.at[k], zout_r.at[k], comp=y * 4 + p)

    def lon_to_right():
        return remote(pack_r, halo_l, lon_s.at[0], lon_r.at[0], grid=g_right)

    def lon_to_left():
        return remote(pack_l, halo_r, lon_s.at[1], lon_r.at[1], grid=g_left)

    for i in range(4):
        load(i).start()

    barrier = pltpu.get_barrier_semaphore()
    for dz in (1, 2, 3):
        pl.semaphore_signal(barrier, inc=1, device_id={"comp": y * 4 + zpeer(dz)}, device_id_type=MESH)
    pl.semaphore_signal(barrier, inc=1, device_id={"comp": y_up}, device_id_type=MESH)
    pl.semaphore_signal(barrier, inc=1, device_id={"comp": y_dn}, device_id_type=MESH)
    pl.semaphore_signal(barrier, inc=1, device_id={"grid": g_right}, device_id_type=MESH)
    pl.semaphore_signal(barrier, inc=1, device_id={"grid": g_left}, device_id_type=MESH)

    def lanes(i):
        return slice(ORDER[i] * LANES, (ORDER[i] + 1) * LANES)

    def rows8(rg):
        return pl.ds(pl.multiple_of(rg * 8, 8), 8)

    def prepare(i):
        load(i).wait()
        for dz in (2, 1, 3, 0):
            rg = zpeer(dz)
            sea = mk[rows8(rg), lanes(i)].astype(f32)

            @pl.loop(0, NTH // JB)
            def _(b):
                at = pl.ds(b * JB, JB)
                piece = xbuf[i, at, rows8(rg)] * sea[None]
                sbuf[i, rg, at] = piece
                if dz == 0:
                    ebuf[i, 4 + z, at] = piece

            if i == 0 and dz == 2:
                pl.semaphore_wait(barrier, 7)
            if i == 0 and dz:
                zin(i, dz).start()
        send_halo(i, z)

    wind_w = tab[2, me]
    inv_cel = tab[3, me]
    courant = tab[4, me]

    def grow(i):
        for rg in range(4):
            speed = uw[rg * 8 : rg * 8 + 8, lanes(i)] * inv_cel
            head = wd[rg * 8 : rg * 8 + 8, lanes(i)]
            along, across = speed * jnp.cos(head), speed * jnp.sin(head)

            @pl.loop(0, NTH, unroll=4)
            def _(j):
                growth = wind_w * jnp.maximum(0.0, tab[0, j] * along + tab[1, j] * across - 1.0)
                post[i, rg, j] = sbuf[i, rg, j] * (1.0 + growth)

    def constants():
        row = lax.broadcasted_iota(jnp.int32, (LAT, LANES), 0).astype(f32)

        def cosine(offset):
            return jnp.cos((BAND_CENTRE + (row - offset) * CELL_DEGREES) * (math.pi / 180.0))

        inverse = 1.0 / cosine((LAT - 1) / 2.0)
        rowinv[...] = inverse
        facehi[...] = cosine(LAT / 2.0 - 1.0) * inverse
        facelo[...] = cosine(LAT / 2.0) * inverse
        for i in range(4):
            if WINDOW[i]:
                above[i, 0] = jnp.zeros((NTH, 8, LANES), f32)
            else:
                below[i, 3] = jnp.zeros((NTH, 8, LANES), f32)

    def send_halo(i, f):
        halo_each(i, f, lambda: hal_up(i, f).start(), lambda: hal_dn(i, f).start())

    def forward(i):
        for dz in (1, 2, 3):
            zin(i, dz).wait_recv()
            if i < 3:
                zin(i + 1, dz).start()
            send_halo(i, zfrom(dz))

    def interact(i):
        for f in halo_ups(i):
            hal_up(i, f).wait_recv()
        for f in halo_dns(i):
            hal_dn(i, f).wait_recv()
        w = WINDOW[i]

        @pl.loop(0, 4)
        def _(k):
            beyond = k >= 4 - w
            low = jnp.where(beyond, has_hi, 1.0)
            lo_a = jnp.where(k < 4 - w, has_lo, low) * D1W
            lo_b = jnp.where(k < 3 - w, has_lo, low) * D0W
            hi_a = jnp.where((k >= 2 - w) & ~beyond, has_hi, 1.0) * U0
            hi_b = jnp.where((k >= 1 - w) & ~beyond, has_hi, 1.0) * U1

            @pl.loop(0, NTH // JB)
            def _(b):
                at = pl.ds(b * JB, JB)
                to = pl.ds(b * JB + PAD, JB)
                eux[to] = hi_a * ebuf[i, k + w + 6, at] + hi_b * ebuf[i, k + w + 7, at]
                edx[to] = lo_b * ebuf[i, k + w + 1, at] + lo_a * ebuf[i, k + w, at]

            for ref in (eux, edx):
                ref[0:PAD] = ref[NTH : NTH + PAD]
                ref[NTH + PAD : NTH + 2 * PAD] = ref[PAD : 2 * PAD]

            @pl.loop(0, NTH // JB)
            def _(b):
                def eu(o):
                    return eux[pl.ds(b * JB + PAD + o, JB)]

                def ed(o):
                    return edx[pl.ds(b * JB + PAD + o, JB)]

                e = ebuf[i, k + w + 4, pl.ds(b * JB, JB)]

                def delta(plus, minus):
                    return e * (e * (W_UP * plus + W_DOWN * minus) - W_CROSS * plus * minus)

                to = pl.ds(b * JB + PAD, JB)
                d1x[to] = delta(N0 * eu(1) + N1 * eu(2), F0 * ed(-3) + F1 * ed(-4))
                d2x[to] = delta(N0 * eu(-1) + N1 * eu(-2), F0 * ed(3) + F1 * ed(4))

            for ref in (d1x, d2x):
                ref[0:PAD] = ref[NTH : NTH + PAD]
                ref[NTH + PAD : NTH + 2 * PAD] = ref[PAD : 2 * PAD]

            @pl.loop(0, NTH // JB)
            def _(b):
                def a1(o):
                    return d1x[pl.ds(b * JB + PAD + o, JB)]

                def a2(o):
                    return d2x[pl.ds(b * JB + PAD + o, JB)]

                at = pl.ds(b * JB, JB)
                bus[k, at] = N0 * (a1(-1) + a2(1)) + N1 * (a1(-2) + a2(2))
                bds[k, at] = F0 * (a1(3) + a2(-3)) + F1 * (a1(4) + a2(-4))
                cen[k, at] = -2.0 * (a1(0) + a2(0))

        @pl.loop(0, NTH)
        def _(j):
            bd = [bds[k, j] for k in range(4)]
            bu = [bus[k, j] for k in range(4)]
            ce = [cen[k, j] for k in range(4)]
            if w:
                own = has_hi * bd[3]
                tbuf[i, 1, j] = D1W * bd[0]
                tbuf[i, 2, j] = D0W * bd[0] + D1W * bd[1]
                tbuf[i, 3, j] = D0W * bd[1] + D1W * bd[2]
                tbuf[i, 4, j] = D0W * bd[2] + D1W * own
                tbuf[i, 5, j] = ce[0] + D0W * own
                tbuf[i, 6, j] = ce[1]
                tbuf[i, 7, j] = ce[2] + U0 * bu[0]
                tbuf[i, 8, j] = ce[3] + has_hi * (U1 * bu[0] + U0 * bu[1])
                tbuf[i, 9, j] = has_hi * (U1 * bu[1] + U0 * bu[2])
                tbuf[i, 10, j] = has_hi * (U1 * bu[2]) + U0 * bu[3]
                tbuf[i, 11, j] = U1 * bu[3]
            else:
                tbuf[i, 0, j] = D1W * bd[0]
                tbuf[i, 1, j] = D0W * bd[0] + D1W * bd[1]
                tbuf[i, 2, j] = D0W * bd[1] + D1W * bd[2]
                tbuf[i, 3, j] = D0W * bd[2] + D1W * bd[3]
                tbuf[i, 4, j] = ce[0] + D0W * bd[3]
                tbuf[i, 5, j] = ce[1]
                tbuf[i, 6, j] = ce[2] + U0 * bu[0]
                tbuf[i, 7, j] = ce[3] + U1 * bu[0] + U0 * bu[1]
                tbuf[i, 8, j] = U1 * bu[1] + U0 * bu[2]
                tbuf[i, 9, j] = U1 * bu[2] + U0 * bu[3]
                tbuf[i, 10, j] = U1 * bu[3]

        for dz in (1, 2, 3, 0):
            m = zpeer(dz)
            back_each(i, m, lambda: bak_up(i, m).start(), lambda: bak_dn(i, m).start())

    def gather(i, half=0):
        at = part(i, half)
        for dz in (1, 2, 3, 0):
            m = zpeer(dz)
            more = i == 3 and half == 0

            def up():
                bak_up(i, m, half).wait_recv()
                if more:
                    bak_up(i, m, 1).start()

            def down():
                bak_dn(i, m, half).wait_recv()
                if more:
                    bak_dn(i, m, 1).start()

            back_each(i, m, up, down)
            under = 1.0 if WINDOW[i] else has_lo
            total = tbuf[i, 4 + m, at] + has_hi * above[i, m, at] + under * below[i, m, at]
            if dz == 0:
                ibuf[i, z, at] = total
            else:
                incr[i, m, at] = total
                zout(i, dz, half).start()

    def finish(i, half=0):
        for dz in (1, 2, 3):
            zout(i, dz, half).wait_recv()
        whole = part(i, half).size

        @pl.loop(0, whole // 6)
        def _(b):
            at = pl.ds(half * HALF + b * 6, 6)
            for rg in range(4):
                post[i, rg, at] = post[i, rg, at] + ibuf[i, rg, at]

    lane = lax.broadcasted_iota(jnp.int32, (8, LANES), 1)

    def edges():
        first, last = ORDER.index(0), ORDER.index(3)

        @pl.loop(0, 4)
        def _(rg):
            a, b = post[first, rg, 0], pltpu.roll(post[last, rg, 0], 2, 1)
            for j in range(1, NTH):
                here = lane >= 2 * j
                a = jnp.where(here, pltpu.roll(post[first, rg, j], 2 * j, 1), a)
                b = jnp.where(here, pltpu.roll(post[last, rg, j], 2 * j + 2, 1), b)
            pack_l[rg] = a
            pack_r[rg] = b

        lon_to_right().start()
        lon_to_left().start()

    sub = lax.broadcasted_iota(jnp.int32, (8, LANES), 0)

    def shift(here, other, by, axis):
        size = LANES if axis else 8
        place = lane if axis else sub
        if by > 0:
            return pltpu.roll(jnp.where(place >= size - by, other, here), by, axis)
        return pltpu.roll(jnp.where(place < -by, other, here), size + by, axis)

    def sweep_x(c, v, left, right, positive):
        c = c if positive else -c
        q = (1.0 - c * c) * (1.0 / 6.0)
        mid = 0.5 + 0.5 * c + 2.0 * q
        far = 0.5 - 0.5 * c - q
        k_next, k_here = c * far, 1.0 - c * (mid - far)
        k_back, k_back2 = c * (q + mid), c * q
        outs = []
        for here, low, high in zip(v, left, right, strict=True):
            up, dn = (low, high) if positive else (high, low)
            way = 1 if positive else -1
            nxt = shift(here, dn, -way, 1)
            back = shift(here, up, way, 1)
            back2 = shift(here, up, 2 * way, 1)
            outs.append(k_here * here - k_next * nxt + k_back * back - k_back2 * back2)
        return outs

    def sweep_y(c, u, positive):
        q = (1.0 - c * c) * (1.0 / 6.0)
        zero = jnp.zeros((8, LANES), f32)
        tiles = [zero, *u, zero]
        faces = []
        if positive:
            t_back, t_here, t_next = -q * c, c * (0.5 + 0.5 * c + 2.0 * q), c * (0.5 - 0.5 * c - q)
        else:
            t_here, t_next, t_next2 = c * (0.5 + 0.5 * c - q), c * (0.5 - 0.5 * c + 2.0 * q), -q * c
        for r in range(5):
            here = tiles[r]
            high = tiles[r + 1]
            face = t_here * here + t_next * shift(here, high, -1, 0)
            if positive:
                if r:
                    face = face + t_back * shift(here, tiles[r - 1], 1, 0)
            else:
                face = face + t_next2 * shift(here, high, -2, 0)
            faces.append(face)
        outs = []
        for r in range(4):
            over, under = faces[r + 1], shift(faces[r + 1], faces[r], 1, 0)
            at = slice(r * 8, r * 8 + 8)
            outs.append(u[r] - (facehi[at] * over - facelo[at] * under))
        return outs

    def propagate(chunks, half):
        @pl.loop(0, NTH // 4)
        def _(t):
            for quarter in (2 * half, 2 * half + 1):
                j = t + 9 * quarter
                x_pos, y_pos = quarter in (0, 3), quarter in (0, 1)
                swept = [[None] * 4 for _ in chunks]
                for rg in range(4):
                    v = {col: post[ORDER.index(col), rg, j] for col in range(4)}
                    if 0 in chunks:
                        v[-1] = has_left * pltpu.roll(halo_l[rg], 126 - 2 * j, 1)
                    if 3 in chunks:
                        v[4] = has_right * pltpu.roll(halo_r[rg], LANES - 2 * j, 1)
                    outs = sweep_x(
                        (courant * tab[0, j]) * rowinv[rg * 8 : rg * 8 + 8],
                        [v[col] for col in chunks],
                        [v[col - 1] for col in chunks],
                        [v[col + 1] for col in chunks],
                        x_pos,
                    )
                    for n, out in enumerate(outs):
                        sea = mk[rg * 8 : rg * 8 + 8, lanes(ORDER.index(chunks[n]))]
                        swept[n][rg] = out * sea.astype(f32)
                for n, col in enumerate(chunks):
                    outs = sweep_y(courant * tab[1, j], swept[n], y_pos)
                    for rg in range(4):
                        at = slice(rg * 8, rg * 8 + 8)
                        sea = mk[at, lanes(ORDER.index(col))].astype(f32)
                        obuf[ORDER.index(col), j, at] = outs[rg] * sea

        for col in chunks:
            store(ORDER.index(col), half).start()

    for i in range(4):
        prepare(i)
    constants()
    grow(0)
    forward(0)
    grow(1)
    forward(1)
    interact(0)
    grow(2)
    forward(2)
    interact(1)
    grow(3)
    gather(0)
    forward(3)
    interact(2)
    gather(1)
    interact(3)
    finish(0)
    gather(2)
    finish(1)
    edges()
    gather(3, 0)
    gather(3, 1)
    finish(2)
    lon_to_right().wait_recv()
    lon_to_left().wait_recv()
    propagate((0,), 0)
    propagate((0,), 1)
    finish(3, 0)
    propagate((1, 2, 3), 0)
    finish(3, 1)
    propagate((1, 2, 3), 1)

    for i in range(4):
        for dz in (1, 2, 3):
            zin(i, dz).wait_send()
        for f in halo_ups(i):
            hal_up(i, f).wait_send()
        for f in halo_dns(i):
            hal_dn(i, f).wait_send()
        for half in range(2 if i == 3 else 1):
            for dz in (1, 2, 3):
                zout(i, dz, half).wait_send()
            for m in back_ups(i):
                bak_up(i, m, half).wait_send()
            for m in back_dns(i):
                bak_dn(i, m, half).wait_send()
        store(i, 0).wait()
        store(i, 1).wait()
    lon_to_right().wait_send()
    lon_to_left().wait_send()


def shards(spectra, u_wind, wind_dir, sea_mask):
    f32 = jnp.float32
    tile = (NTH, 8, LANES)
    vmem, dma = pltpu.VMEM, pltpu.SemaphoreType.DMA
    inner = pl.BlockSpec(memory_space=pltpu.VMEM)
    columns = jnp.transpose(spectra, (0, 2, 1, 3))
    result = pl.pallas_call(
        kernel,
        out_shape=jax.ShapeDtypeStruct(columns.shape, f32),
        in_specs=[
            pl.BlockSpec(memory_space=pltpu.SMEM),
            pl.BlockSpec(memory_space=pltpu.HBM),
            inner, inner, inner,
        ],
        out_specs=pl.BlockSpec(memory_space=pl.ANY),
        scratch_shapes=[
            vmem((4, NTH, LAT, LANES), f32),
            vmem((4, NTH, LAT, LANES), f32),
            vmem((4, 4) + tile, f32),
            vmem((4, 12) + tile, f32),
            vmem((4, 12) + tile, f32),
            vmem((4, 4) + tile, f32),
            vmem((4, 4) + tile, f32),
            vmem((4, 4) + tile, f32),
            vmem((4, 4) + tile, f32),
            vmem((4, 4) + tile, f32),
            vmem((NTH + 2 * PAD, 8, LANES), f32),
            vmem((NTH + 2 * PAD, 8, LANES), f32),
            vmem((NTH + 2 * PAD, 8, LANES), f32),
            vmem((NTH + 2 * PAD, 8, LANES), f32),
            vmem((4,) + tile, f32),
            vmem((4,) + tile, f32),
            vmem((4,) + tile, f32),
            vmem((LAT, LANES), f32),
            vmem((LAT, LANES), f32),
            vmem((LAT, LANES), f32),
            vmem((4, 8, LANES), f32),
            vmem((4, 8, LANES), f32),
            vmem((4, 8, LANES), f32),
            vmem((4, 8, LANES), f32),
            dma((4,)), dma((8,)),
            dma((16,)), dma((16,)),
            dma((32,)), dma((32,)),
            dma((40,)), dma((40,)),
            dma((20,)), dma((20,)),
            dma((2,)), dma((2,)),
        ],
        compiler_params=pltpu.CompilerParams(
            collective_id=0, has_side_effects=True, vmem_limit_bytes=50 << 20
        ),
        cost_estimate=pl.CostEstimate(flops=60_000_000, bytes_accessed=5_000_000, transcendentals=32_768),
        name="wave_step",
    )(tables(), columns, u_wind, wind_dir, sea_mask)
    return jnp.transpose(result, (0, 2, 1, 3))


def solution(mesh):
    return jax.shard_map(
        shards,
        mesh=mesh,
        in_specs=(P("comp", None, None, "grid"), P(None, "grid"), P(None, "grid"), P(None, "grid")),
        out_specs=P("comp", None, None, "grid"),
        check_vma=False,
    )
```

```python
import math

import numpy as np

import jax
import jax.numpy as jnp
from jax import lax
from jax.experimental import pallas as pl
from jax.experimental.pallas import tpu as pltpu
from jax.sharding import PartitionSpec as P

MESH = pl.DeviceIdType.MESH
NK, NTH, LAT = 32, 36, 32
GRAVITY = 9.81
LAMBDA = 0.25
WIND = 0.0003125 * 120.0
ADVECT_STEP = 220.0
EARTH_RADIUS = 6371000.0
BAND_CENTRE = 30.0
CELL_DEGREES = 0.05
CELL_RADIANS = CELL_DEGREES * math.pi / 180.0
SHIFT_UP = math.log(1.0 + LAMBDA) / math.log(1.1)
SHIFT_DOWN = math.log(1.0 - LAMBDA) / math.log(1.1)
NEAR = 11.48 * NTH / 360.0
FAR = 33.56 * NTH / 360.0
U1 = SHIFT_UP - 2.0
U0 = 1.0 - U1
D1W = -SHIFT_DOWN - 3.0
D0W = 1.0 - D1W
N1 = NEAR - 1.0
N0 = 1.0 - N1
F1 = FAR - 3.0
F0 = 1.0 - F1
W_UP = 0.1 / (1.0 + LAMBDA) ** 4
W_DOWN = 0.1 / (1.0 - LAMBDA) ** 4
W_CROSS = 0.2 / (1.0 - LAMBDA * LAMBDA) ** 4

ORDER = (0, 3, 1, 2)
WINDOW = (0, 1, 0, 1)
LANES = 128
HALF = NTH // 2
JB = 4
PAD = 4


def tables():
    t = np.zeros((8, 128), np.float64)
    th = 2.0 * np.pi * np.arange(NTH) / NTH
    t[0, :NTH] = np.cos(th)
    t[1, :NTH] = np.sin(th)
    f = 0.04 * 1.1 ** np.arange(NK)
    w = 2.0 * np.pi * f
    t[2, :NK] = WIND * w
    t[3, :NK] = w / GRAVITY
    t[4, :NK] = GRAVITY / (2.0 * w) * ADVECT_STEP / (EARTH_RADIUS * CELL_RADIANS)
    return t.astype(np.float32)


def halo_ups(i):
    return range(1, 4) if WINDOW[i] else range(4)


def halo_dns(i):
    return range(4) if WINDOW[i] else range(3)


def back_ups(i):
    return range(4) if WINDOW[i] else range(3)


def back_dns(i):
    return range(1, 4) if WINDOW[i] else range(4)


def kernel(
    tab_hbm, x_hbm, uw_hbm, wd_hbm, mk_hbm, o_hbm,
    tab, uw, wd, mk, xbuf, obuf, sbuf, ebuf, tbuf, above, below, incr, ibuf, post,
    eux, edx, d1x, d2x, bus, bds, cen, rowinv, facehi, facelo,
    pack_l, pack_r, halo_l, halo_r,
    load_s, store_s, cell_s, zin_s, zin_r, hal_s, hal_r, bak_s, bak_r, zout_s, zout_r, lon_s, lon_r,
):
    f32 = jnp.float32
    me = lax.axis_index("comp")
    g = lax.axis_index("grid")
    y, z = me // 4, lax.rem(me, 4)
    y_up = lax.rem(y + 1, 8) * 4 + z
    y_dn = lax.rem(y + 7, 8) * 4 + z
    g_right, g_left = lax.rem(g + 1, 16), lax.rem(g + 15, 16)
    has_lo = jnp.where(y > 0, 1.0, 0.0).astype(f32)
    has_hi = jnp.where(y < 7, 1.0, 0.0).astype(f32)
    has_left = jnp.where(g > 0, 1.0, 0.0).astype(f32)
    has_right = jnp.where(g < 15, 1.0, 0.0).astype(f32)

    def zpeer(dz):
        return lax.rem(z + dz, 4)

    def zfrom(dz):
        return lax.rem(z + 4 - dz, 4)

    def load(i):
        return pltpu.make_async_copy(
            x_hbm.at[0, :, :, pl.ds(ORDER[i] * LANES, LANES)], xbuf.at[i], load_s.at[i]
        )

    def store(i, half):
        at = pl.ds(half * HALF, HALF)
        return pltpu.make_async_copy(
            obuf.at[i, at], o_hbm.at[0, at, :, pl.ds(ORDER[i] * LANES, LANES)], store_s.at[i * 2 + half]
        )

    def travels(i, f, four, action):
        if four:
            action()
        else:

            @pl.when(f >= 1 if WINDOW[i] else f < 3)
            def _():
                action()

    def halo_each(i, f, up, down):
        travels(i, f, WINDOW[i] == 0, up)
        travels(i, f, WINDOW[i] == 1, down)

    def back_each(i, m, up, down):
        travels(i, m, WINDOW[i] == 1, up)
        travels(i, m, WINDOW[i] == 0, down)

    def part(i, half):
        return pl.ds(half * HALF, HALF) if i == 3 else pl.ds(0, NTH)

    def remote(src, dst, ss, rs, **to):
        return pltpu.make_async_remote_copy(
            src_ref=src, dst_ref=dst, send_sem=ss, recv_sem=rs, device_id=to, device_id_type=MESH
        )

    def zin(i, dz):
        p = zpeer(dz)
        k = i * 4 + dz
        return remote(sbuf.at[i, p], ebuf.at[i, 4 + z], zin_s.at[k], zin_r.at[k], comp=y * 4 + p)

    def hal_up(i, f):
        k = i * 8 + f
        return remote(ebuf.at[i, 4 + f], ebuf.at[i, f], hal_s.at[k], hal_r.at[k], comp=y_up)

    def hal_dn(i, f):
        k = i * 8 + 4 + f
        return remote(ebuf.at[i, 4 + f], ebuf.at[i, 8 + f], hal_s.at[k], hal_r.at[k], comp=y_dn)

    def bak_dn(i, m, half=0):
        k, at = (i + half) * 8 + m, part(i, half)
        return remote(tbuf.at[i, m, at], above.at[i, m, at], bak_s.at[k], bak_r.at[k], comp=y_dn)

    def bak_up(i, m, half=0):
        k, at = (i + half) * 8 + 4 + m, part(i, half)
        return remote(tbuf.at[i, 8 + m, at], below.at[i, m, at], bak_s.at[k], bak_r.at[k], comp=y_up)

    def zout(i, dz, half=0):
        p, at = zpeer(dz), part(i, half)
        k = (i + half) * 4 + dz
        return remote(incr.at[i, p, at], ibuf.at[i, z, at], zout_s.at[k], zout_r.at[k], comp=y * 4 + p)

    def lon_to_right():
        return remote(pack_r, halo_l, lon_s.at[0], lon_r.at[0], grid=g_right)

    def lon_to_left():
        return remote(pack_l, halo_r, lon_s.at[1], lon_r.at[1], grid=g_left)

    cells = [
        pltpu.make_async_copy(src, dst, cell_s.at[n])
        for n, (src, dst) in enumerate(
            ((mk_hbm, mk), (uw_hbm, uw), (wd_hbm, wd), (tab_hbm, tab))
        )
    ]
    cells[0].start()
    for i in range(4):
        load(i).start()
    for n in (3, 1, 2):
        cells[n].start()

    barrier = pltpu.get_barrier_semaphore()
    for dz in (1, 2, 3):
        pl.semaphore_signal(barrier, inc=1, device_id={"comp": y * 4 + zpeer(dz)}, device_id_type=MESH)
    pl.semaphore_signal(barrier, inc=1, device_id={"comp": y_up}, device_id_type=MESH)
    pl.semaphore_signal(barrier, inc=1, device_id={"comp": y_dn}, device_id_type=MESH)
    pl.semaphore_signal(barrier, inc=1, device_id={"grid": g_right}, device_id_type=MESH)
    pl.semaphore_signal(barrier, inc=1, device_id={"grid": g_left}, device_id_type=MESH)

    def lanes(i):
        return slice(ORDER[i] * LANES, (ORDER[i] + 1) * LANES)

    def rows8(rg):
        return pl.ds(pl.multiple_of(rg * 8, 8), 8)

    def prepare(i):
        load(i).wait()
        for dz in (2, 1, 3, 0):
            rg = zpeer(dz)
            sea = mk[rows8(rg), lanes(i)].astype(f32)

            @pl.loop(0, NTH // JB)
            def _(b):
                at = pl.ds(b * JB, JB)
                piece = xbuf[i, at, rows8(rg)] * sea[None]
                sbuf[i, rg, at] = piece
                if dz == 0:
                    ebuf[i, 4 + z, at] = piece

            if i == 0 and dz == 2:
                pl.semaphore_wait(barrier, 7)
            if i == 0 and dz:
                zin(i, dz).start()
        send_halo(i, z)


    def grow(i):
        for rg in range(4):
            speed = uw[rg * 8 : rg * 8 + 8, lanes(i)] * inv_cel
            head = wd[rg * 8 : rg * 8 + 8, lanes(i)]
            along, across = speed * jnp.cos(head), speed * jnp.sin(head)

            @pl.loop(0, NTH, unroll=4)
            def _(j):
                growth = wind_w * jnp.maximum(0.0, tab[0, j] * along + tab[1, j] * across - 1.0)
                post[i, rg, j] = sbuf[i, rg, j] * (1.0 + growth)

    def constants():
        row = lax.broadcasted_iota(jnp.int32, (LAT, LANES), 0).astype(f32)

        def cosine(offset):
            return jnp.cos((BAND_CENTRE + (row - offset) * CELL_DEGREES) * (math.pi / 180.0))

        inverse = 1.0 / cosine((LAT - 1) / 2.0)
        rowinv[...] = inverse
        facehi[...] = cosine(LAT / 2.0 - 1.0) * inverse
        facelo[...] = cosine(LAT / 2.0) * inverse
        for i in range(4):
            if WINDOW[i]:
                above[i, 0] = jnp.zeros((NTH, 8, LANES), f32)
            else:
                below[i, 3] = jnp.zeros((NTH, 8, LANES), f32)

    def send_halo(i, f):
        halo_each(i, f, lambda: hal_up(i, f).start(), lambda: hal_dn(i, f).start())

    def forward(i):
        for dz in (1, 2, 3):
            zin(i, dz).wait_recv()
            if i < 3:
                zin(i + 1, dz).start()
            send_halo(i, zfrom(dz))

    def interact(i):
        for f in halo_ups(i):
            hal_up(i, f).wait_recv()
        for f in halo_dns(i):
            hal_dn(i, f).wait_recv()
        w = WINDOW[i]

        @pl.loop(0, 4)
        def _(k):
            beyond = k >= 4 - w
            low = jnp.where(beyond, has_hi, 1.0)
            lo_a = jnp.where(k < 4 - w, has_lo, low) * D1W
            lo_b = jnp.where(k < 3 - w, has_lo, low) * D0W
            hi_a = jnp.where((k >= 2 - w) & ~beyond, has_hi, 1.0) * U0
            hi_b = jnp.where((k >= 1 - w) & ~beyond, has_hi, 1.0) * U1

            @pl.loop(0, NTH // JB)
            def _(b):
                at = pl.ds(b * JB, JB)
                to = pl.ds(b * JB + PAD, JB)
                eux[to] = hi_a * ebuf[i, k + w + 6, at] + hi_b * ebuf[i, k + w + 7, at]
                edx[to] = lo_b * ebuf[i, k + w + 1, at] + lo_a * ebuf[i, k + w, at]

            for ref in (eux, edx):
                ref[0:PAD] = ref[NTH : NTH + PAD]
                ref[NTH + PAD : NTH + 2 * PAD] = ref[PAD : 2 * PAD]

            @pl.loop(0, NTH // JB)
            def _(b):
                def eu(o):
                    return eux[pl.ds(b * JB + PAD + o, JB)]

                def ed(o):
                    return edx[pl.ds(b * JB + PAD + o, JB)]

                e = ebuf[i, k + w + 4, pl.ds(b * JB, JB)]

                def delta(plus, minus):
                    return e * (e * (W_UP * plus + W_DOWN * minus) - W_CROSS * plus * minus)

                to = pl.ds(b * JB + PAD, JB)
                d1x[to] = delta(N0 * eu(1) + N1 * eu(2), F0 * ed(-3) + F1 * ed(-4))
                d2x[to] = delta(N0 * eu(-1) + N1 * eu(-2), F0 * ed(3) + F1 * ed(4))

            for ref in (d1x, d2x):
                ref[0:PAD] = ref[NTH : NTH + PAD]
                ref[NTH + PAD : NTH + 2 * PAD] = ref[PAD : 2 * PAD]

            @pl.loop(0, NTH // JB)
            def _(b):
                def a1(o):
                    return d1x[pl.ds(b * JB + PAD + o, JB)]

                def a2(o):
                    return d2x[pl.ds(b * JB + PAD + o, JB)]

                at = pl.ds(b * JB, JB)
                bus[k, at] = N0 * (a1(-1) + a2(1)) + N1 * (a1(-2) + a2(2))
                bds[k, at] = F0 * (a1(3) + a2(-3)) + F1 * (a1(4) + a2(-4))
                cen[k, at] = -2.0 * (a1(0) + a2(0))

        @pl.loop(0, NTH)
        def _(j):
            bd = [bds[k, j] for k in range(4)]
            bu = [bus[k, j] for k in range(4)]
            ce = [cen[k, j] for k in range(4)]
            if w:
                own = has_hi * bd[3]
                tbuf[i, 1, j] = D1W * bd[0]
                tbuf[i, 2, j] = D0W * bd[0] + D1W * bd[1]
                tbuf[i, 3, j] = D0W * bd[1] + D1W * bd[2]
                tbuf[i, 4, j] = D0W * bd[2] + D1W * own
                tbuf[i, 5, j] = ce[0] + D0W * own
                tbuf[i, 6, j] = ce[1]
                tbuf[i, 7, j] = ce[2] + U0 * bu[0]
                tbuf[i, 8, j] = ce[3] + has_hi * (U1 * bu[0] + U0 * bu[1])
                tbuf[i, 9, j] = has_hi * (U1 * bu[1] + U0 * bu[2])
                tbuf[i, 10, j] = has_hi * (U1 * bu[2]) + U0 * bu[3]
                tbuf[i, 11, j] = U1 * bu[3]
            else:
                tbuf[i, 0, j] = D1W * bd[0]
                tbuf[i, 1, j] = D0W * bd[0] + D1W * bd[1]
                tbuf[i, 2, j] = D0W * bd[1] + D1W * bd[2]
                tbuf[i, 3, j] = D0W * bd[2] + D1W * bd[3]
                tbuf[i, 4, j] = ce[0] + D0W * bd[3]
                tbuf[i, 5, j] = ce[1]
                tbuf[i, 6, j] = ce[2] + U0 * bu[0]
                tbuf[i, 7, j] = ce[3] + U1 * bu[0] + U0 * bu[1]
                tbuf[i, 8, j] = U1 * bu[1] + U0 * bu[2]
                tbuf[i, 9, j] = U1 * bu[2] + U0 * bu[3]
                tbuf[i, 10, j] = U1 * bu[3]

        for dz in (1, 2, 3, 0):
            m = zpeer(dz)
            back_each(i, m, lambda: bak_up(i, m).start(), lambda: bak_dn(i, m).start())

    def gather(i, half=0):
        at = part(i, half)
        for dz in (1, 2, 3, 0):
            m = zpeer(dz)
            more = i == 3 and half == 0

            def up():
                bak_up(i, m, half).wait_recv()
                if more:
                    bak_up(i, m, 1).start()

            def down():
                bak_dn(i, m, half).wait_recv()
                if more:
                    bak_dn(i, m, 1).start()

            back_each(i, m, up, down)
            under = 1.0 if WINDOW[i] else has_lo
            total = tbuf[i, 4 + m, at] + has_hi * above[i, m, at] + under * below[i, m, at]
            if dz == 0:
                ibuf[i, z, at] = total
            else:
                incr[i, m, at] = total
                zout(i, dz, half).start()

    def finish(i, half=0):
        for dz in (1, 2, 3):
            zout(i, dz, half).wait_recv()
        whole = part(i, half).size

        @pl.loop(0, whole // 6)
        def _(b):
            at = pl.ds(half * HALF + b * 6, 6)
            for rg in range(4):
                post[i, rg, at] = post[i, rg, at] + ibuf[i, rg, at]

    lane = lax.broadcasted_iota(jnp.int32, (8, LANES), 1)

    def edges():
        first, last = ORDER.index(0), ORDER.index(3)

        @pl.loop(0, 4)
        def _(rg):
            a, b = post[first, rg, 0], pltpu.roll(post[last, rg, 0], 2, 1)
            for j in range(1, NTH):
                here = lane >= 2 * j
                a = jnp.where(here, pltpu.roll(post[first, rg, j], 2 * j, 1), a)
                b = jnp.where(here, pltpu.roll(post[last, rg, j], 2 * j + 2, 1), b)
            pack_l[rg] = a
            pack_r[rg] = b

        lon_to_right().start()
        lon_to_left().start()

    sub = lax.broadcasted_iota(jnp.int32, (8, LANES), 0)

    def shift(here, other, by, axis):
        size = LANES if axis else 8
        place = lane if axis else sub
        if by > 0:
            return pltpu.roll(jnp.where(place >= size - by, other, here), by, axis)
        return pltpu.roll(jnp.where(place < -by, other, here), size + by, axis)

    def sweep_x(c, v, left, right, positive):
        c = c if positive else -c
        q = (1.0 - c * c) * (1.0 / 6.0)
        mid = 0.5 + 0.5 * c + 2.0 * q
        far = 0.5 - 0.5 * c - q
        k_next, k_here = c * far, 1.0 - c * (mid - far)
        k_back, k_back2 = c * (q + mid), c * q
        outs = []
        for here, low, high in zip(v, left, right, strict=True):
            up, dn = (low, high) if positive else (high, low)
            way = 1 if positive else -1
            nxt = shift(here, dn, -way, 1)
            back = shift(here, up, way, 1)
            back2 = shift(here, up, 2 * way, 1)
            outs.append(k_here * here - k_next * nxt + k_back * back - k_back2 * back2)
        return outs

    def sweep_y(c, u, positive):
        q = (1.0 - c * c) * (1.0 / 6.0)
        zero = jnp.zeros((8, LANES), f32)
        tiles = [zero, *u, zero]
        faces = []
        if positive:
            t_back, t_here, t_next = -q * c, c * (0.5 + 0.5 * c + 2.0 * q), c * (0.5 - 0.5 * c - q)
        else:
            t_here, t_next, t_next2 = c * (0.5 + 0.5 * c - q), c * (0.5 - 0.5 * c + 2.0 * q), -q * c
        for r in range(5):
            here = tiles[r]
            high = tiles[r + 1]
            face = t_here * here + t_next * shift(here, high, -1, 0)
            if positive:
                if r:
                    face = face + t_back * shift(here, tiles[r - 1], 1, 0)
            else:
                face = face + t_next2 * shift(here, high, -2, 0)
            faces.append(face)
        outs = []
        for r in range(4):
            over, under = faces[r + 1], shift(faces[r + 1], faces[r], 1, 0)
            at = slice(r * 8, r * 8 + 8)
            outs.append(u[r] - (facehi[at] * over - facelo[at] * under))
        return outs

    def propagate(chunks, half):
        @pl.loop(0, NTH // 4)
        def _(t):
            for quarter in (2 * half, 2 * half + 1):
                j = t + 9 * quarter
                x_pos, y_pos = quarter in (0, 3), quarter in (0, 1)
                swept = [[None] * 4 for _ in chunks]
                for rg in range(4):
                    v = {col: post[ORDER.index(col), rg, j] for col in range(4)}
                    if 0 in chunks:
                        v[-1] = has_left * pltpu.roll(halo_l[rg], 126 - 2 * j, 1)
                    if 3 in chunks:
                        v[4] = has_right * pltpu.roll(halo_r[rg], LANES - 2 * j, 1)
                    outs = sweep_x(
                        (courant * tab[0, j]) * rowinv[rg * 8 : rg * 8 + 8],
                        [v[col] for col in chunks],
                        [v[col - 1] for col in chunks],
                        [v[col + 1] for col in chunks],
                        x_pos,
                    )
                    for n, out in enumerate(outs):
                        sea = mk[rg * 8 : rg * 8 + 8, lanes(ORDER.index(chunks[n]))]
                        swept[n][rg] = out * sea.astype(f32)
                for n, col in enumerate(chunks):
                    outs = sweep_y(courant * tab[1, j], swept[n], y_pos)
                    for rg in range(4):
                        at = slice(rg * 8, rg * 8 + 8)
                        sea = mk[at, lanes(ORDER.index(col))].astype(f32)
                        obuf[ORDER.index(col), j, at] = outs[rg] * sea

        for col in chunks:
            store(ORDER.index(col), half).start()

    cells[0].wait()
    for i in range(4):
        prepare(i)
    constants()
    for n in (1, 2, 3):
        cells[n].wait()
    wind_w, inv_cel, courant = tab[2, me], tab[3, me], tab[4, me]
    grow(0)
    forward(0)
    grow(1)
    forward(1)
    interact(0)
    grow(2)
    forward(2)
    interact(1)
    grow(3)
    gather(0)
    forward(3)
    interact(2)
    gather(1)
    interact(3)
    finish(0)
    gather(2)
    finish(1)
    edges()
    gather(3, 0)
    gather(3, 1)
    finish(2)
    lon_to_right().wait_recv()
    lon_to_left().wait_recv()
    propagate((0,), 0)
    propagate((0,), 1)
    finish(3, 0)
    propagate((1, 2, 3), 0)
    finish(3, 1)
    propagate((1, 2, 3), 1)

    for i in range(4):
        for dz in (1, 2, 3):
            zin(i, dz).wait_send()
        for f in halo_ups(i):
            hal_up(i, f).wait_send()
        for f in halo_dns(i):
            hal_dn(i, f).wait_send()
        for half in range(2 if i == 3 else 1):
            for dz in (1, 2, 3):
                zout(i, dz, half).wait_send()
            for m in back_ups(i):
                bak_up(i, m, half).wait_send()
            for m in back_dns(i):
                bak_dn(i, m, half).wait_send()
        store(i, 0).wait()
        store(i, 1).wait()
    lon_to_right().wait_send()
    lon_to_left().wait_send()


def shards(spectra, u_wind, wind_dir, sea_mask):
    f32 = jnp.float32
    tile = (NTH, 8, LANES)
    vmem, dma = pltpu.VMEM, pltpu.SemaphoreType.DMA
    outer = pl.BlockSpec(memory_space=pltpu.HBM)
    shape = u_wind.shape
    def stay(a):
        return pltpu.with_memory_space_constraint(a, pltpu.HBM)

    columns = jnp.transpose(spectra, (0, 2, 1, 3))
    result = pl.pallas_call(
        kernel,
        out_shape=jax.ShapeDtypeStruct(columns.shape, f32),
        in_specs=[
            outer, outer, outer, outer, outer,
        ],
        out_specs=pl.BlockSpec(memory_space=pl.ANY),
        scratch_shapes=[
            pltpu.SMEM((8, 128), f32),
            vmem(shape, f32), vmem(shape, f32), vmem(shape, jnp.int32),
            vmem((4, NTH, LAT, LANES), f32),
            vmem((4, NTH, LAT, LANES), f32),
            vmem((4, 4) + tile, f32),
            vmem((4, 12) + tile, f32),
            vmem((4, 12) + tile, f32),
            vmem((4, 4) + tile, f32),
            vmem((4, 4) + tile, f32),
            vmem((4, 4) + tile, f32),
            vmem((4, 4) + tile, f32),
            vmem((4, 4) + tile, f32),
            vmem((NTH + 2 * PAD, 8, LANES), f32),
            vmem((NTH + 2 * PAD, 8, LANES), f32),
            vmem((NTH + 2 * PAD, 8, LANES), f32),
            vmem((NTH + 2 * PAD, 8, LANES), f32),
            vmem((4,) + tile, f32),
            vmem((4,) + tile, f32),
            vmem((4,) + tile, f32),
            vmem((LAT, LANES), f32),
            vmem((LAT, LANES), f32),
            vmem((LAT, LANES), f32),
            vmem((4, 8, LANES), f32),
            vmem((4, 8, LANES), f32),
            vmem((4, 8, LANES), f32),
            vmem((4, 8, LANES), f32),
            dma((4,)), dma((8,)), dma((4,)),
            dma((16,)), dma((16,)),
            dma((32,)), dma((32,)),
            dma((40,)), dma((40,)),
            dma((20,)), dma((20,)),
            dma((2,)), dma((2,)),
        ],
        compiler_params=pltpu.CompilerParams(
            collective_id=0, has_side_effects=True, vmem_limit_bytes=50 << 20
        ),
        cost_estimate=pl.CostEstimate(flops=60_000_000, bytes_accessed=5_000_000, transcendentals=32_768),
        name="wave_step",
    )(*(stay(a) for a in (jnp.asarray(tables()), columns, u_wind, wind_dir, sea_mask)))
    return jnp.transpose(result, (0, 2, 1, 3))


def solution(mesh):
    return jax.shard_map(
        shards,
        mesh=mesh,
        in_specs=(P("comp", None, None, "grid"), P(None, "grid"), P(None, "grid"), P(None, "grid")),
        out_specs=P("comp", None, None, "grid"),
        check_vma=False,
    )
```

```python
import math

import numpy as np

import jax
import jax.numpy as jnp
from jax import lax
from jax.experimental import pallas as pl
from jax.experimental.pallas import tpu as pltpu
from jax.sharding import PartitionSpec as P

MESH = pl.DeviceIdType.MESH
NK, NTH, LAT = 32, 36, 32
GRAVITY = 9.81
LAMBDA = 0.25
WIND = 0.0003125 * 120.0
ADVECT_STEP = 220.0
EARTH_RADIUS = 6371000.0
BAND_CENTRE = 30.0
CELL_DEGREES = 0.05
CELL_RADIANS = CELL_DEGREES * math.pi / 180.0
SHIFT_UP = math.log(1.0 + LAMBDA) / math.log(1.1)
SHIFT_DOWN = math.log(1.0 - LAMBDA) / math.log(1.1)
NEAR = 11.48 * NTH / 360.0
FAR = 33.56 * NTH / 360.0
U1 = SHIFT_UP - 2.0
U0 = 1.0 - U1
D1W = -SHIFT_DOWN - 3.0
D0W = 1.0 - D1W
N1 = NEAR - 1.0
N0 = 1.0 - N1
F1 = FAR - 3.0
F0 = 1.0 - F1
W_UP = 0.1 / (1.0 + LAMBDA) ** 4
W_DOWN = 0.1 / (1.0 - LAMBDA) ** 4
W_CROSS = 0.2 / (1.0 - LAMBDA * LAMBDA) ** 4

ORDER = (0, 3, 1, 2)
WINDOW = (0, 1, 0, 1)
LANES = 128
HALF = NTH // 2
JB = 4
PAD = 4


def tables():
    t = np.zeros((8, 128), np.float64)
    th = 2.0 * np.pi * np.arange(NTH) / NTH
    t[0, :NTH] = np.cos(th)
    t[1, :NTH] = np.sin(th)
    f = 0.04 * 1.1 ** np.arange(NK)
    w = 2.0 * np.pi * f
    t[2, :NK] = WIND * w
    t[3, :NK] = w / GRAVITY
    t[4, :NK] = GRAVITY / (2.0 * w) * ADVECT_STEP / (EARTH_RADIUS * CELL_RADIANS)
    return t.astype(np.float32)


def halo_ups(i):
    return range(1, 4) if WINDOW[i] else range(4)


def halo_dns(i):
    return range(4) if WINDOW[i] else range(3)


def back_ups(i):
    return range(4) if WINDOW[i] else range(3)


def back_dns(i):
    return range(1, 4) if WINDOW[i] else range(4)


def kernel(
    tab_hbm, x_hbm, uw_hbm, wd_hbm, mk_hbm, o_hbm,
    tab, uw, wd, mk, xbuf, obuf, sbuf, ebuf, tbuf, above, below, incr, ibuf, post,
    eux, edx, d1x, d2x, bus, bds, cen, rowinv, facehi, facelo,
    pack_l, pack_r, halo_l, halo_r,
    load_s, store_s, cell_s, zin_s, zin_r, hal_s, hal_r, bak_s, bak_r, zout_s, zout_r, lon_s, lon_r,
):
    f32 = jnp.float32
    me = lax.axis_index("comp")
    g = lax.axis_index("grid")
    y, z = me // 4, lax.rem(me, 4)
    y_up = lax.rem(y + 1, 8) * 4 + z
    y_dn = lax.rem(y + 7, 8) * 4 + z
    g_right, g_left = lax.rem(g + 1, 16), lax.rem(g + 15, 16)
    has_lo = jnp.where(y > 0, 1.0, 0.0).astype(f32)
    has_hi = jnp.where(y < 7, 1.0, 0.0).astype(f32)
    has_left = jnp.where(g > 0, 1.0, 0.0).astype(f32)
    has_right = jnp.where(g < 15, 1.0, 0.0).astype(f32)

    def zpeer(dz):
        return lax.rem(z + dz, 4)

    def zfrom(dz):
        return lax.rem(z + 4 - dz, 4)

    def load(i):
        return pltpu.make_async_copy(
            x_hbm.at[0, :, :, pl.ds(ORDER[i] * LANES, LANES)], xbuf.at[i], load_s.at[i]
        )

    def store(i, quarter):
        at = pl.ds(quarter * (NTH // 4), NTH // 4)
        return pltpu.make_async_copy(
            obuf.at[i, at], o_hbm.at[0, at, :, pl.ds(ORDER[i] * LANES, LANES)], store_s.at[i * 4 + quarter]
        )

    def travels(i, f, four, action):
        if four:
            action()
        else:

            @pl.when(f >= 1 if WINDOW[i] else f < 3)
            def _():
                action()

    def halo_each(i, f, up, down):
        travels(i, f, WINDOW[i] == 0, up)
        travels(i, f, WINDOW[i] == 1, down)

    def back_each(i, m, up, down):
        travels(i, m, WINDOW[i] == 1, up)
        travels(i, m, WINDOW[i] == 0, down)

    def part(i, half):
        return pl.ds(half * HALF, HALF) if i == 3 else pl.ds(0, NTH)

    def remote(src, dst, ss, rs, **to):
        return pltpu.make_async_remote_copy(
            src_ref=src, dst_ref=dst, send_sem=ss, recv_sem=rs, device_id=to, device_id_type=MESH
        )

    def zin(i, dz):
        p = zpeer(dz)
        k = i * 4 + dz
        return remote(sbuf.at[i, p], ebuf.at[i, 4 + z], zin_s.at[k], zin_r.at[k], comp=y * 4 + p)

    def hal_up(i, f):
        k = i * 8 + f
        return remote(ebuf.at[i, 4 + f], ebuf.at[i, f], hal_s.at[k], hal_r.at[k], comp=y_up)

    def hal_dn(i, f):
        k = i * 8 + 4 + f
        return remote(ebuf.at[i, 4 + f], ebuf.at[i, 8 + f], hal_s.at[k], hal_r.at[k], comp=y_dn)

    def bak_dn(i, m, half=0):
        k, at = (i + half) * 8 + m, part(i, half)
        return remote(tbuf.at[i, m, at], above.at[i, m, at], bak_s.at[k], bak_r.at[k], comp=y_dn)

    def bak_up(i, m, half=0):
        k, at = (i + half) * 8 + 4 + m, part(i, half)
        return remote(tbuf.at[i, 8 + m, at], below.at[i, m, at], bak_s.at[k], bak_r.at[k], comp=y_up)

    def zout(i, dz, half=0):
        p, at = zpeer(dz), part(i, half)
        k = (i + half) * 4 + dz
        return remote(incr.at[i, p, at], ibuf.at[i, z, at], zout_s.at[k], zout_r.at[k], comp=y * 4 + p)

    def lon_to_right():
        return remote(pack_r, halo_l, lon_s.at[0], lon_r.at[0], grid=g_right)

    def lon_to_left():
        return remote(pack_l, halo_r, lon_s.at[1], lon_r.at[1], grid=g_left)

    cells = [
        pltpu.make_async_copy(src, dst, cell_s.at[n])
        for n, (src, dst) in enumerate(
            ((mk_hbm, mk), (uw_hbm, uw), (wd_hbm, wd), (tab_hbm, tab))
        )
    ]
    cells[0].start()
    for i in range(4):
        load(i).start()
    for n in (3, 1, 2):
        cells[n].start()

    barrier = pltpu.get_barrier_semaphore()
    for dz in (1, 2, 3):
        pl.semaphore_signal(barrier, inc=1, device_id={"comp": y * 4 + zpeer(dz)}, device_id_type=MESH)
    pl.semaphore_signal(barrier, inc=1, device_id={"comp": y_up}, device_id_type=MESH)
    pl.semaphore_signal(barrier, inc=1, device_id={"comp": y_dn}, device_id_type=MESH)
    pl.semaphore_signal(barrier, inc=1, device_id={"grid": g_right}, device_id_type=MESH)
    pl.semaphore_signal(barrier, inc=1, device_id={"grid": g_left}, device_id_type=MESH)

    def lanes(i):
        return slice(ORDER[i] * LANES, (ORDER[i] + 1) * LANES)

    def rows8(rg):
        return pl.ds(pl.multiple_of(rg * 8, 8), 8)

    def prepare(i):
        load(i).wait()
        for dz in (2, 1, 3, 0):
            rg = zpeer(dz)
            sea = mk[rows8(rg), lanes(i)].astype(f32)

            @pl.loop(0, NTH // JB)
            def _(b):
                at = pl.ds(b * JB, JB)
                piece = xbuf[i, at, rows8(rg)] * sea[None]
                sbuf[i, rg, at] = piece
                if dz == 0:
                    ebuf[i, 4 + z, at] = piece

            if i == 0 and dz == 2:
                pl.semaphore_wait(barrier, 7)
            if i == 0 and dz:
                zin(i, dz).start()
        send_halo(i, z)


    def grow(i):
        for rg in range(4):
            speed = uw[rg * 8 : rg * 8 + 8, lanes(i)] * inv_cel
            head = wd[rg * 8 : rg * 8 + 8, lanes(i)]
            along, across = speed * jnp.cos(head), speed * jnp.sin(head)

            @pl.loop(0, NTH, unroll=4)
            def _(j):
                growth = wind_w * jnp.maximum(0.0, tab[0, j] * along + tab[1, j] * across - 1.0)
                post[i, rg, j] = sbuf[i, rg, j] * (1.0 + growth)

    def constants():
        row = lax.broadcasted_iota(jnp.int32, (LAT, LANES), 0).astype(f32)

        def cosine(offset):
            return jnp.cos((BAND_CENTRE + (row - offset) * CELL_DEGREES) * (math.pi / 180.0))

        inverse = 1.0 / cosine((LAT - 1) / 2.0)
        rowinv[...] = inverse
        facehi[...] = cosine(LAT / 2.0 - 1.0) * inverse
        facelo[...] = cosine(LAT / 2.0) * inverse
        for i in range(4):
            if WINDOW[i]:
                above[i, 0] = jnp.zeros((NTH, 8, LANES), f32)
            else:
                below[i, 3] = jnp.zeros((NTH, 8, LANES), f32)

    def send_halo(i, f):
        halo_each(i, f, lambda: hal_up(i, f).start(), lambda: hal_dn(i, f).start())

    def forward(i):
        for dz in (1, 2, 3):
            zin(i, dz).wait_recv()
            if i < 3:
                zin(i + 1, dz).start()
            send_halo(i, zfrom(dz))

    def interact(i):
        for f in halo_ups(i):
            hal_up(i, f).wait_recv()
        for f in halo_dns(i):
            hal_dn(i, f).wait_recv()
        w = WINDOW[i]

        @pl.loop(0, 4)
        def _(k):
            beyond = k >= 4 - w
            low = jnp.where(beyond, has_hi, 1.0)
            lo_a = jnp.where(k < 4 - w, has_lo, low) * D1W
            lo_b = jnp.where(k < 3 - w, has_lo, low) * D0W
            hi_a = jnp.where((k >= 2 - w) & ~beyond, has_hi, 1.0) * U0
            hi_b = jnp.where((k >= 1 - w) & ~beyond, has_hi, 1.0) * U1

            @pl.loop(0, NTH // JB)
            def _(b):
                at = pl.ds(b * JB, JB)
                to = pl.ds(b * JB + PAD, JB)
                eux[to] = hi_a * ebuf[i, k + w + 6, at] + hi_b * ebuf[i, k + w + 7, at]
                edx[to] = lo_b * ebuf[i, k + w + 1, at] + lo_a * ebuf[i, k + w, at]

            for ref in (eux, edx):
                ref[0:PAD] = ref[NTH : NTH + PAD]
                ref[NTH + PAD : NTH + 2 * PAD] = ref[PAD : 2 * PAD]

            @pl.loop(0, NTH // JB)
            def _(b):
                def eu(o):
                    return eux[pl.ds(b * JB + PAD + o, JB)]

                def ed(o):
                    return edx[pl.ds(b * JB + PAD + o, JB)]

                e = ebuf[i, k + w + 4, pl.ds(b * JB, JB)]

                def delta(plus, minus):
                    return e * (e * (W_UP * plus + W_DOWN * minus) - W_CROSS * plus * minus)

                to = pl.ds(b * JB + PAD, JB)
                d1x[to] = delta(N0 * eu(1) + N1 * eu(2), F0 * ed(-3) + F1 * ed(-4))
                d2x[to] = delta(N0 * eu(-1) + N1 * eu(-2), F0 * ed(3) + F1 * ed(4))

            for ref in (d1x, d2x):
                ref[0:PAD] = ref[NTH : NTH + PAD]
                ref[NTH + PAD : NTH + 2 * PAD] = ref[PAD : 2 * PAD]

            @pl.loop(0, NTH // JB)
            def _(b):
                def a1(o):
                    return d1x[pl.ds(b * JB + PAD + o, JB)]

                def a2(o):
                    return d2x[pl.ds(b * JB + PAD + o, JB)]

                at = pl.ds(b * JB, JB)
                bus[k, at] = N0 * (a1(-1) + a2(1)) + N1 * (a1(-2) + a2(2))
                bds[k, at] = F0 * (a1(3) + a2(-3)) + F1 * (a1(4) + a2(-4))
                cen[k, at] = -2.0 * (a1(0) + a2(0))

        @pl.loop(0, NTH)
        def _(j):
            bd = [bds[k, j] for k in range(4)]
            bu = [bus[k, j] for k in range(4)]
            ce = [cen[k, j] for k in range(4)]
            if w:
                own = has_hi * bd[3]
                tbuf[i, 1, j] = D1W * bd[0]
                tbuf[i, 2, j] = D0W * bd[0] + D1W * bd[1]
                tbuf[i, 3, j] = D0W * bd[1] + D1W * bd[2]
                tbuf[i, 4, j] = D0W * bd[2] + D1W * own
                tbuf[i, 5, j] = ce[0] + D0W * own
                tbuf[i, 6, j] = ce[1]
                tbuf[i, 7, j] = ce[2] + U0 * bu[0]
                tbuf[i, 8, j] = ce[3] + has_hi * (U1 * bu[0] + U0 * bu[1])
                tbuf[i, 9, j] = has_hi * (U1 * bu[1] + U0 * bu[2])
                tbuf[i, 10, j] = has_hi * (U1 * bu[2]) + U0 * bu[3]
                tbuf[i, 11, j] = U1 * bu[3]
            else:
                tbuf[i, 0, j] = D1W * bd[0]
                tbuf[i, 1, j] = D0W * bd[0] + D1W * bd[1]
                tbuf[i, 2, j] = D0W * bd[1] + D1W * bd[2]
                tbuf[i, 3, j] = D0W * bd[2] + D1W * bd[3]
                tbuf[i, 4, j] = ce[0] + D0W * bd[3]
                tbuf[i, 5, j] = ce[1]
                tbuf[i, 6, j] = ce[2] + U0 * bu[0]
                tbuf[i, 7, j] = ce[3] + U1 * bu[0] + U0 * bu[1]
                tbuf[i, 8, j] = U1 * bu[1] + U0 * bu[2]
                tbuf[i, 9, j] = U1 * bu[2] + U0 * bu[3]
                tbuf[i, 10, j] = U1 * bu[3]

        for dz in (1, 2, 3, 0):
            m = zpeer(dz)
            back_each(i, m, lambda: bak_up(i, m).start(), lambda: bak_dn(i, m).start())

    def gather(i, half=0):
        at = part(i, half)
        for dz in (1, 2, 3, 0):
            m = zpeer(dz)
            more = i == 3 and half == 0

            def up():
                bak_up(i, m, half).wait_recv()
                if more:
                    bak_up(i, m, 1).start()

            def down():
                bak_dn(i, m, half).wait_recv()
                if more:
                    bak_dn(i, m, 1).start()

            back_each(i, m, up, down)
            under = 1.0 if WINDOW[i] else has_lo
            total = tbuf[i, 4 + m, at] + has_hi * above[i, m, at] + under * below[i, m, at]
            if dz == 0:
                ibuf[i, z, at] = total
            else:
                incr[i, m, at] = total
                zout(i, dz, half).start()

    def finish(i, half=0):
        for dz in (1, 2, 3):
            zout(i, dz, half).wait_recv()
        whole = part(i, half).size

        @pl.loop(0, whole // 6)
        def _(b):
            at = pl.ds(half * HALF + b * 6, 6)
            for rg in range(4):
                post[i, rg, at] = post[i, rg, at] + ibuf[i, rg, at]

    lane = lax.broadcasted_iota(jnp.int32, (8, LANES), 1)

    def edges():
        first, last = ORDER.index(0), ORDER.index(3)

        @pl.loop(0, 4)
        def _(rg):
            a, b = post[first, rg, 0], pltpu.roll(post[last, rg, 0], 2, 1)
            for j in range(1, NTH):
                here = lane >= 2 * j
                a = jnp.where(here, pltpu.roll(post[first, rg, j], 2 * j, 1), a)
                b = jnp.where(here, pltpu.roll(post[last, rg, j], 2 * j + 2, 1), b)
            pack_l[rg] = a
            pack_r[rg] = b

        lon_to_right().start()
        lon_to_left().start()

    sub = lax.broadcasted_iota(jnp.int32, (8, LANES), 0)

    def shift(here, other, by, axis):
        size = LANES if axis else 8
        place = lane if axis else sub
        if by > 0:
            return pltpu.roll(jnp.where(place >= size - by, other, here), by, axis)
        return pltpu.roll(jnp.where(place < -by, other, here), size + by, axis)

    def sweep_x(c, v, left, right, positive):
        c = c if positive else -c
        q = (1.0 - c * c) * (1.0 / 6.0)
        mid = 0.5 + 0.5 * c + 2.0 * q
        far = 0.5 - 0.5 * c - q
        k_next, k_here = c * far, 1.0 - c * (mid - far)
        k_back, k_back2 = c * (q + mid), c * q
        outs = []
        for here, low, high in zip(v, left, right, strict=True):
            up, dn = (low, high) if positive else (high, low)
            way = 1 if positive else -1
            nxt = shift(here, dn, -way, 1)
            back = shift(here, up, way, 1)
            back2 = shift(here, up, 2 * way, 1)
            outs.append(k_here * here - k_next * nxt + k_back * back - k_back2 * back2)
        return outs

    def sweep_y(c, u, positive):
        q = (1.0 - c * c) * (1.0 / 6.0)
        zero = jnp.zeros((8, LANES), f32)
        tiles = [zero, *u, zero]
        faces = []
        if positive:
            t_back, t_here, t_next = -q * c, c * (0.5 + 0.5 * c + 2.0 * q), c * (0.5 - 0.5 * c - q)
        else:
            t_here, t_next, t_next2 = c * (0.5 + 0.5 * c - q), c * (0.5 - 0.5 * c + 2.0 * q), -q * c
        for r in range(5):
            here = tiles[r]
            high = tiles[r + 1]
            face = t_here * here + t_next * shift(here, high, -1, 0)
            if positive:
                if r:
                    face = face + t_back * shift(here, tiles[r - 1], 1, 0)
            else:
                face = face + t_next2 * shift(here, high, -2, 0)
            faces.append(face)
        outs = []
        for r in range(4):
            over, under = faces[r + 1], shift(faces[r + 1], faces[r], 1, 0)
            at = slice(r * 8, r * 8 + 8)
            outs.append(u[r] - (facehi[at] * over - facelo[at] * under))
        return outs

    def propagate(chunks, quarters):
        @pl.loop(0, NTH // 4)
        def _(t):
            for quarter in quarters:
                j = t + 9 * quarter
                x_pos, y_pos = quarter in (0, 3), quarter in (0, 1)
                swept = [[None] * 4 for _ in chunks]
                for rg in range(4):
                    v = {col: post[ORDER.index(col), rg, j] for col in range(4)}
                    if 0 in chunks:
                        v[-1] = has_left * pltpu.roll(halo_l[rg], 126 - 2 * j, 1)
                    if 3 in chunks:
                        v[4] = has_right * pltpu.roll(halo_r[rg], LANES - 2 * j, 1)
                    outs = sweep_x(
                        (courant * tab[0, j]) * rowinv[rg * 8 : rg * 8 + 8],
                        [v[col] for col in chunks],
                        [v[col - 1] for col in chunks],
                        [v[col + 1] for col in chunks],
                        x_pos,
                    )
                    for n, out in enumerate(outs):
                        sea = mk[rg * 8 : rg * 8 + 8, lanes(ORDER.index(chunks[n]))]
                        swept[n][rg] = out * sea.astype(f32)
                for n, col in enumerate(chunks):
                    outs = sweep_y(courant * tab[1, j], swept[n], y_pos)
                    for rg in range(4):
                        at = slice(rg * 8, rg * 8 + 8)
                        sea = mk[at, lanes(ORDER.index(col))].astype(f32)
                        obuf[ORDER.index(col), j, at] = outs[rg] * sea

        for col in chunks:
            for quarter in quarters:
                store(ORDER.index(col), quarter).start()

    cells[0].wait()
    for i in range(4):
        prepare(i)
    constants()
    for n in (1, 2, 3):
        cells[n].wait()
    wind_w, inv_cel, courant = tab[2, me], tab[3, me], tab[4, me]
    grow(0)
    forward(0)
    grow(1)
    forward(1)
    interact(0)
    grow(2)
    forward(2)
    interact(1)
    grow(3)
    gather(0)
    forward(3)
    interact(2)
    gather(1)
    interact(3)
    gather(2)
    finish(0)
    gather(3, 0)
    finish(1)
    edges()
    gather(3, 1)
    finish(2)
    lon_to_right().wait_recv()
    lon_to_left().wait_recv()
    propagate((0,), (0, 1))
    propagate((0,), (2, 3))
    finish(3, 0)
    propagate((1, 2, 3), (0, 1))
    finish(3, 1)
    propagate((1, 2, 3), (2,))
    propagate((1, 2, 3), (3,))

    for i in range(4):
        for dz in (1, 2, 3):
            zin(i, dz).wait_send()
        for f in halo_ups(i):
            hal_up(i, f).wait_send()
        for f in halo_dns(i):
            hal_dn(i, f).wait_send()
        for half in range(2 if i == 3 else 1):
            for dz in (1, 2, 3):
                zout(i, dz, half).wait_send()
            for m in back_ups(i):
                bak_up(i, m, half).wait_send()
            for m in back_dns(i):
                bak_dn(i, m, half).wait_send()
        for quarter in range(4):
            store(i, quarter).wait()
    lon_to_right().wait_send()
    lon_to_left().wait_send()


def shards(spectra, u_wind, wind_dir, sea_mask):
    f32 = jnp.float32
    tile = (NTH, 8, LANES)
    vmem, dma = pltpu.VMEM, pltpu.SemaphoreType.DMA
    outer = pl.BlockSpec(memory_space=pltpu.HBM)
    shape = u_wind.shape
    def stay(a):
        return pltpu.with_memory_space_constraint(a, pltpu.HBM)

    columns = jnp.transpose(spectra, (0, 2, 1, 3))
    result = pl.pallas_call(
        kernel,
        out_shape=jax.ShapeDtypeStruct(columns.shape, f32),
        in_specs=[
            outer, outer, outer, outer, outer,
        ],
        out_specs=pl.BlockSpec(memory_space=pl.ANY),
        scratch_shapes=[
            pltpu.SMEM((8, 128), f32),
            vmem(shape, f32), vmem(shape, f32), vmem(shape, jnp.int32),
            vmem((4, NTH, LAT, LANES), f32),
            vmem((4, NTH, LAT, LANES), f32),
            vmem((4, 4) + tile, f32),
            vmem((4, 12) + tile, f32),
            vmem((4, 12) + tile, f32),
            vmem((4, 4) + tile, f32),
            vmem((4, 4) + tile, f32),
            vmem((4, 4) + tile, f32),
            vmem((4, 4) + tile, f32),
            vmem((4, 4) + tile, f32),
            vmem((NTH + 2 * PAD, 8, LANES), f32),
            vmem((NTH + 2 * PAD, 8, LANES), f32),
            vmem((NTH + 2 * PAD, 8, LANES), f32),
            vmem((NTH + 2 * PAD, 8, LANES), f32),
            vmem((4,) + tile, f32),
            vmem((4,) + tile, f32),
            vmem((4,) + tile, f32),
            vmem((LAT, LANES), f32),
            vmem((LAT, LANES), f32),
            vmem((LAT, LANES), f32),
            vmem((4, 8, LANES), f32),
            vmem((4, 8, LANES), f32),
            vmem((4, 8, LANES), f32),
            vmem((4, 8, LANES), f32),
            dma((4,)), dma((16,)), dma((4,)),
            dma((16,)), dma((16,)),
            dma((32,)), dma((32,)),
            dma((40,)), dma((40,)),
            dma((20,)), dma((20,)),
            dma((2,)), dma((2,)),
        ],
        compiler_params=pltpu.CompilerParams(
            collective_id=0, has_side_effects=True, vmem_limit_bytes=50 << 20
        ),
        cost_estimate=pl.CostEstimate(flops=60_000_000, bytes_accessed=5_000_000, transcendentals=32_768),
        name="wave_step",
    )(*(stay(a) for a in (jnp.asarray(tables()), columns, u_wind, wind_dir, sea_mask)))
    return jnp.transpose(result, (0, 2, 1, 3))


def solution(mesh):
    return jax.shard_map(
        shards,
        mesh=mesh,
        in_specs=(P("comp", None, None, "grid"), P(None, "grid"), P(None, "grid"), P(None, "grid")),
        out_specs=P("comp", None, None, "grid"),
        check_vma=False,
    )
```

```python
import math

import numpy as np

import jax
import jax.numpy as jnp
from jax import lax
from jax.experimental import pallas as pl
from jax.experimental.pallas import tpu as pltpu
from jax.sharding import PartitionSpec as P

MESH = pl.DeviceIdType.MESH
NK, NTH, LAT = 32, 36, 32
GRAVITY = 9.81
LAMBDA = 0.25
WIND = 0.0003125 * 120.0
ADVECT_STEP = 220.0
EARTH_RADIUS = 6371000.0
BAND_CENTRE = 30.0
CELL_DEGREES = 0.05
CELL_RADIANS = CELL_DEGREES * math.pi / 180.0
SHIFT_UP = math.log(1.0 + LAMBDA) / math.log(1.1)
SHIFT_DOWN = math.log(1.0 - LAMBDA) / math.log(1.1)
NEAR = 11.48 * NTH / 360.0
FAR = 33.56 * NTH / 360.0
U1 = SHIFT_UP - 2.0
U0 = 1.0 - U1
D1W = -SHIFT_DOWN - 3.0
D0W = 1.0 - D1W
N1 = NEAR - 1.0
N0 = 1.0 - N1
F1 = FAR - 3.0
F0 = 1.0 - F1
W_UP = 0.1 / (1.0 + LAMBDA) ** 4
W_DOWN = 0.1 / (1.0 - LAMBDA) ** 4
W_CROSS = 0.2 / (1.0 - LAMBDA * LAMBDA) ** 4

ORDER = (0, 3, 1, 2)
WINDOW = (0, 1, 0, 1)
LANES = 128
HALF = NTH // 2
JB = 4
PAD = 4


def tables():
    t = np.zeros((8, 128), np.float64)
    th = 2.0 * np.pi * np.arange(NTH) / NTH
    t[0, :NTH] = np.cos(th)
    t[1, :NTH] = np.sin(th)
    f = 0.04 * 1.1 ** np.arange(NK)
    w = 2.0 * np.pi * f
    t[2, :NK] = WIND * w
    t[3, :NK] = w / GRAVITY
    t[4, :NK] = GRAVITY / (2.0 * w) * ADVECT_STEP / (EARTH_RADIUS * CELL_RADIANS)
    return t.astype(np.float32)


def halo_ups(i):
    return range(1, 4) if WINDOW[i] else range(4)


def halo_dns(i):
    return range(4) if WINDOW[i] else range(3)


def back_ups(i):
    return range(4) if WINDOW[i] else range(3)


def back_dns(i):
    return range(1, 4) if WINDOW[i] else range(4)


def kernel(
    tab_hbm, x_hbm, uw_hbm, wd_hbm, mk_hbm, o_hbm,
    tab, uw, wd, mk, xbuf, obuf, sbuf, ebuf, tbuf, above, below, incr, ibuf, post,
    eux, edx, d1x, d2x, bus, bds, cen, rowinv, facehi, facelo,
    pack_l, pack_r, halo_l, halo_r,
    load_s, store_s, cell_s, zin_s, zin_r, hal_s, hal_r, bak_s, bak_r, zout_s, zout_r, lon_s, lon_r,
):
    f32 = jnp.float32
    me = lax.axis_index("comp")
    g = lax.axis_index("grid")
    y, z = me // 4, lax.rem(me, 4)
    y_up = lax.rem(y + 1, 8) * 4 + z
    y_dn = lax.rem(y + 7, 8) * 4 + z
    g_right, g_left = lax.rem(g + 1, 16), lax.rem(g + 15, 16)
    has_lo = jnp.where(y > 0, 1.0, 0.0).astype(f32)
    has_hi = jnp.where(y < 7, 1.0, 0.0).astype(f32)
    has_left = jnp.where(g > 0, 1.0, 0.0).astype(f32)
    has_right = jnp.where(g < 15, 1.0, 0.0).astype(f32)

    def zpeer(dz):
        return lax.rem(z + dz, 4)

    def zfrom(dz):
        return lax.rem(z + 4 - dz, 4)

    def load(i):
        return pltpu.make_async_copy(
            x_hbm.at[0, :, :, pl.ds(ORDER[i] * LANES, LANES)], xbuf.at[i], load_s.at[i]
        )

    def store(i, quarter):
        at = pl.ds(quarter * (NTH // 4), NTH // 4)
        return pltpu.make_async_copy(
            obuf.at[i, at], o_hbm.at[0, at, :, pl.ds(ORDER[i] * LANES, LANES)], store_s.at[i * 4 + quarter]
        )

    def travels(i, f, four, action):
        if four:
            action()
        else:

            @pl.when(f >= 1 if WINDOW[i] else f < 3)
            def _():
                action()

    def halo_each(i, f, up, down):
        travels(i, f, WINDOW[i] == 0, up)
        travels(i, f, WINDOW[i] == 1, down)

    def back_each(i, m, up, down):
        travels(i, m, WINDOW[i] == 1, up)
        travels(i, m, WINDOW[i] == 0, down)

    def part(i, half):
        return pl.ds(half * HALF, HALF) if i == 3 else pl.ds(0, NTH)

    def remote(src, dst, ss, rs, **to):
        return pltpu.make_async_remote_copy(
            src_ref=src, dst_ref=dst, send_sem=ss, recv_sem=rs, device_id=to, device_id_type=MESH
        )

    def zin(i, dz):
        p = zpeer(dz)
        k = i * 4 + dz
        return remote(sbuf.at[i, p], ebuf.at[i, 4 + z], zin_s.at[k], zin_r.at[k], comp=y * 4 + p)

    def hal_up(i, f):
        k = i * 8 + f
        return remote(ebuf.at[i, 4 + f], ebuf.at[i, f], hal_s.at[k], hal_r.at[k], comp=y_up)

    def hal_dn(i, f):
        k = i * 8 + 4 + f
        return remote(ebuf.at[i, 4 + f], ebuf.at[i, 8 + f], hal_s.at[k], hal_r.at[k], comp=y_dn)

    def bak_dn(i, m, half=0):
        k, at = (i + half) * 8 + m, part(i, half)
        return remote(tbuf.at[i, m, at], above.at[i, m, at], bak_s.at[k], bak_r.at[k], comp=y_dn)

    def bak_up(i, m, half=0):
        k, at = (i + half) * 8 + 4 + m, part(i, half)
        return remote(tbuf.at[i, 8 + m, at], below.at[i, m, at], bak_s.at[k], bak_r.at[k], comp=y_up)

    def zout(i, dz, half=0):
        p, at = zpeer(dz), part(i, half)
        k = (i + half) * 4 + dz
        return remote(incr.at[i, p, at], ibuf.at[i, z, at], zout_s.at[k], zout_r.at[k], comp=y * 4 + p)

    def lon_to_right():
        return remote(pack_r, halo_l, lon_s.at[0], lon_r.at[0], grid=g_right)

    def lon_to_left():
        return remote(pack_l, halo_r, lon_s.at[1], lon_r.at[1], grid=g_left)

    cells = [
        pltpu.make_async_copy(src, dst, cell_s.at[n])
        for n, (src, dst) in enumerate(
            ((mk_hbm, mk), (uw_hbm, uw), (wd_hbm, wd), (tab_hbm, tab))
        )
    ]
    cells[0].start()
    for i in range(4):
        load(i).start()
    for n in (3, 1, 2):
        cells[n].start()

    barrier = pltpu.get_barrier_semaphore()
    for dz in (1, 2, 3):
        pl.semaphore_signal(barrier, inc=1, device_id={"comp": y * 4 + zpeer(dz)}, device_id_type=MESH)
    pl.semaphore_signal(barrier, inc=1, device_id={"comp": y_up}, device_id_type=MESH)
    pl.semaphore_signal(barrier, inc=1, device_id={"comp": y_dn}, device_id_type=MESH)
    pl.semaphore_signal(barrier, inc=1, device_id={"grid": g_right}, device_id_type=MESH)
    pl.semaphore_signal(barrier, inc=1, device_id={"grid": g_left}, device_id_type=MESH)

    def lanes(i):
        return slice(ORDER[i] * LANES, (ORDER[i] + 1) * LANES)

    def rows8(rg):
        return pl.ds(pl.multiple_of(rg * 8, 8), 8)

    def prepare(i):
        load(i).wait()
        for dz in (2, 1, 3, 0):
            rg = zpeer(dz)
            sea = mk[rows8(rg), lanes(i)].astype(f32)

            @pl.loop(0, NTH // JB)
            def _(b):
                at = pl.ds(b * JB, JB)
                piece = xbuf[i, at, rows8(rg)] * sea[None]
                sbuf[i, rg, at] = piece
                if dz == 0:
                    ebuf[i, 4 + z, at] = piece

            if i == 0 and dz == 2:
                pl.semaphore_wait(barrier, 7)
            if i == 0 and dz:
                zin(i, dz).start()
        send_halo(i, z)


    def grow(i):
        for rg in range(4):
            speed = uw[rg * 8 : rg * 8 + 8, lanes(i)] * inv_cel
            head = wd[rg * 8 : rg * 8 + 8, lanes(i)]
            along, across = speed * jnp.cos(head), speed * jnp.sin(head)

            @pl.loop(0, NTH, unroll=4)
            def _(j):
                growth = wind_w * jnp.maximum(0.0, tab[0, j] * along + tab[1, j] * across - 1.0)
                post[i, rg, j] = sbuf[i, rg, j] * (1.0 + growth)

    def constants():
        row = lax.broadcasted_iota(jnp.int32, (LAT, LANES), 0).astype(f32)

        def cosine(offset):
            return jnp.cos((BAND_CENTRE + (row - offset) * CELL_DEGREES) * (math.pi / 180.0))

        inverse = 1.0 / cosine((LAT - 1) / 2.0)
        rowinv[...] = inverse
        facehi[...] = cosine(LAT / 2.0 - 1.0) * inverse
        facelo[...] = cosine(LAT / 2.0) * inverse
        for i in range(4):
            if WINDOW[i]:
                above[i, 0] = jnp.zeros((NTH, 8, LANES), f32)
            else:
                below[i, 3] = jnp.zeros((NTH, 8, LANES), f32)

    def send_halo(i, f):
        halo_each(i, f, lambda: hal_up(i, f).start(), lambda: hal_dn(i, f).start())

    def forward(i):
        for dz in (1, 2, 3):
            zin(i, dz).wait_recv()
            if i < 3:
                zin(i + 1, dz).start()
            send_halo(i, zfrom(dz))

    def interact(i):
        for f in halo_ups(i):
            hal_up(i, f).wait_recv()
        for f in halo_dns(i):
            hal_dn(i, f).wait_recv()
        w = WINDOW[i]

        @pl.loop(0, 4)
        def _(k):
            beyond = k >= 4 - w
            low = jnp.where(beyond, has_hi, 1.0)
            lo_a = jnp.where(k < 4 - w, has_lo, low) * D1W
            lo_b = jnp.where(k < 3 - w, has_lo, low) * D0W
            hi_a = jnp.where((k >= 2 - w) & ~beyond, has_hi, 1.0) * U0
            hi_b = jnp.where((k >= 1 - w) & ~beyond, has_hi, 1.0) * U1

            @pl.loop(0, NTH // JB)
            def _(b):
                at = pl.ds(b * JB, JB)
                to = pl.ds(b * JB + PAD, JB)
                eux[to] = hi_a * ebuf[i, k + w + 6, at] + hi_b * ebuf[i, k + w + 7, at]
                edx[to] = lo_b * ebuf[i, k + w + 1, at] + lo_a * ebuf[i, k + w, at]

            for ref in (eux, edx):
                ref[0:PAD] = ref[NTH : NTH + PAD]
                ref[NTH + PAD : NTH + 2 * PAD] = ref[PAD : 2 * PAD]

            @pl.loop(0, NTH // JB)
            def _(b):
                def eu(o):
                    return eux[pl.ds(b * JB + PAD + o, JB)]

                def ed(o):
                    return edx[pl.ds(b * JB + PAD + o, JB)]

                e = ebuf[i, k + w + 4, pl.ds(b * JB, JB)]

                def delta(plus, minus):
                    return e * (e * (W_UP * plus + W_DOWN * minus) - W_CROSS * plus * minus)

                to = pl.ds(b * JB + PAD, JB)
                d1x[to] = delta(N0 * eu(1) + N1 * eu(2), F0 * ed(-3) + F1 * ed(-4))
                d2x[to] = delta(N0 * eu(-1) + N1 * eu(-2), F0 * ed(3) + F1 * ed(4))

            for ref in (d1x, d2x):
                ref[0:PAD] = ref[NTH : NTH + PAD]
                ref[NTH + PAD : NTH + 2 * PAD] = ref[PAD : 2 * PAD]

            @pl.loop(0, NTH // JB)
            def _(b):
                def a1(o):
                    return d1x[pl.ds(b * JB + PAD + o, JB)]

                def a2(o):
                    return d2x[pl.ds(b * JB + PAD + o, JB)]

                at = pl.ds(b * JB, JB)
                bus[k, at] = N0 * (a1(-1) + a2(1)) + N1 * (a1(-2) + a2(2))
                bds[k, at] = F0 * (a1(3) + a2(-3)) + F1 * (a1(4) + a2(-4))
                cen[k, at] = -2.0 * (a1(0) + a2(0))

        @pl.loop(0, NTH)
        def _(j):
            bd = [bds[k, j] for k in range(4)]
            bu = [bus[k, j] for k in range(4)]
            ce = [cen[k, j] for k in range(4)]
            if w:
                own = has_hi * bd[3]
                tbuf[i, 1, j] = D1W * bd[0]
                tbuf[i, 2, j] = D0W * bd[0] + D1W * bd[1]
                tbuf[i, 3, j] = D0W * bd[1] + D1W * bd[2]
                tbuf[i, 4, j] = D0W * bd[2] + D1W * own
                tbuf[i, 5, j] = ce[0] + D0W * own
                tbuf[i, 6, j] = ce[1]
                tbuf[i, 7, j] = ce[2] + U0 * bu[0]
                tbuf[i, 8, j] = ce[3] + has_hi * (U1 * bu[0] + U0 * bu[1])
                tbuf[i, 9, j] = has_hi * (U1 * bu[1] + U0 * bu[2])
                tbuf[i, 10, j] = has_hi * (U1 * bu[2]) + U0 * bu[3]
                tbuf[i, 11, j] = U1 * bu[3]
            else:
                tbuf[i, 0, j] = D1W * bd[0]
                tbuf[i, 1, j] = D0W * bd[0] + D1W * bd[1]
                tbuf[i, 2, j] = D0W * bd[1] + D1W * bd[2]
                tbuf[i, 3, j] = D0W * bd[2] + D1W * bd[3]
                tbuf[i, 4, j] = ce[0] + D0W * bd[3]
                tbuf[i, 5, j] = ce[1]
                tbuf[i, 6, j] = ce[2] + U0 * bu[0]
                tbuf[i, 7, j] = ce[3] + U1 * bu[0] + U0 * bu[1]
                tbuf[i, 8, j] = U1 * bu[1] + U0 * bu[2]
                tbuf[i, 9, j] = U1 * bu[2] + U0 * bu[3]
                tbuf[i, 10, j] = U1 * bu[3]

        for dz in (1, 2, 3, 0):
            m = zpeer(dz)
            back_each(i, m, lambda: bak_up(i, m).start(), lambda: bak_dn(i, m).start())

    def gather(i, half=0):
        at = part(i, half)
        for dz in (1, 2, 3, 0):
            m = zpeer(dz)
            more = i == 3 and half == 0

            def up():
                bak_up(i, m, half).wait_recv()
                if more:
                    bak_up(i, m, 1).start()

            def down():
                bak_dn(i, m, half).wait_recv()
                if more:
                    bak_dn(i, m, 1).start()

            back_each(i, m, up, down)
            under = 1.0 if WINDOW[i] else has_lo
            total = tbuf[i, 4 + m, at] + has_hi * above[i, m, at] + under * below[i, m, at]
            if dz == 0:
                ibuf[i, z, at] = total
            else:
                incr[i, m, at] = total
                zout(i, dz, half).start()

    def finish(i, half=0):
        for dz in (1, 2, 3):
            zout(i, dz, half).wait_recv()
        whole = part(i, half).size

        @pl.loop(0, whole // 6)
        def _(b):
            at = pl.ds(half * HALF + b * 6, 6)
            for rg in range(4):
                post[i, rg, at] = post[i, rg, at] + ibuf[i, rg, at]

    lane = lax.broadcasted_iota(jnp.int32, (8, LANES), 1)

    def edges():
        first, last = ORDER.index(0), ORDER.index(3)

        @pl.loop(0, 4)
        def _(rg):
            a, b = post[first, rg, 0], pltpu.roll(post[last, rg, 0], 2, 1)
            for j in range(1, NTH):
                here = lane >= 2 * j
                a = jnp.where(here, pltpu.roll(post[first, rg, j], 2 * j, 1), a)
                b = jnp.where(here, pltpu.roll(post[last, rg, j], 2 * j + 2, 1), b)
            pack_l[rg] = a
            pack_r[rg] = b

        lon_to_right().start()
        lon_to_left().start()

    sub = lax.broadcasted_iota(jnp.int32, (8, LANES), 0)

    def shift(here, other, by, axis):
        size = LANES if axis else 8
        place = lane if axis else sub
        if by > 0:
            return pltpu.roll(jnp.where(place >= size - by, other, here), by, axis)
        return pltpu.roll(jnp.where(place < -by, other, here), size + by, axis)

    def sweep_x(c, v, left, right, positive):
        c = c if positive else -c
        q = (1.0 - c * c) * (1.0 / 6.0)
        mid = 0.5 + 0.5 * c + 2.0 * q
        far = 0.5 - 0.5 * c - q
        k_next, k_here = c * far, 1.0 - c * (mid - far)
        k_back, k_back2 = c * (q + mid), c * q
        outs = []
        for here, low, high in zip(v, left, right, strict=True):
            up, dn = (low, high) if positive else (high, low)
            way = 1 if positive else -1
            nxt = shift(here, dn, -way, 1)
            back = shift(here, up, way, 1)
            back2 = shift(here, up, 2 * way, 1)
            outs.append(k_here * here - k_next * nxt + k_back * back - k_back2 * back2)
        return outs

    def sweep_y(c, u, positive):
        q = (1.0 - c * c) * (1.0 / 6.0)
        zero = jnp.zeros((8, LANES), f32)
        tiles = [zero, *u, zero]
        faces = []
        if positive:
            t_back, t_here, t_next = -q * c, c * (0.5 + 0.5 * c + 2.0 * q), c * (0.5 - 0.5 * c - q)
        else:
            t_here, t_next, t_next2 = c * (0.5 + 0.5 * c - q), c * (0.5 - 0.5 * c + 2.0 * q), -q * c
        for r in range(5):
            here = tiles[r]
            high = tiles[r + 1]
            face = t_here * here + t_next * shift(here, high, -1, 0)
            if positive:
                if r:
                    face = face + t_back * shift(here, tiles[r - 1], 1, 0)
            else:
                face = face + t_next2 * shift(here, high, -2, 0)
            faces.append(face)
        outs = []
        for r in range(4):
            over, under = faces[r + 1], shift(faces[r + 1], faces[r], 1, 0)
            at = slice(r * 8, r * 8 + 8)
            outs.append(u[r] - (facehi[at] * over - facelo[at] * under))
        return outs

    def propagate(chunks, quarters):
        @pl.loop(0, NTH // 4)
        def _(t):
            for quarter in quarters:
                j = t + 9 * quarter
                x_pos, y_pos = quarter in (0, 3), quarter in (0, 1)
                swept = [[None] * 4 for _ in chunks]
                for rg in range(4):
                    v = {col: post[ORDER.index(col), rg, j] for col in range(4)}
                    if 0 in chunks:
                        v[-1] = has_left * pltpu.roll(halo_l[rg], 126 - 2 * j, 1)
                    if 3 in chunks:
                        v[4] = has_right * pltpu.roll(halo_r[rg], LANES - 2 * j, 1)
                    outs = sweep_x(
                        (courant * tab[0, j]) * rowinv[rg * 8 : rg * 8 + 8],
                        [v[col] for col in chunks],
                        [v[col - 1] for col in chunks],
                        [v[col + 1] for col in chunks],
                        x_pos,
                    )
                    for n, out in enumerate(outs):
                        sea = mk[rg * 8 : rg * 8 + 8, lanes(ORDER.index(chunks[n]))]
                        swept[n][rg] = out * sea.astype(f32)
                for n, col in enumerate(chunks):
                    outs = sweep_y(courant * tab[1, j], swept[n], y_pos)
                    for rg in range(4):
                        at = slice(rg * 8, rg * 8 + 8)
                        sea = mk[at, lanes(ORDER.index(col))].astype(f32)
                        obuf[ORDER.index(col), j, at] = outs[rg] * sea

        for col in chunks:
            for quarter in quarters:
                store(ORDER.index(col), quarter).start()

    cells[0].wait()
    for i in range(4):
        prepare(i)
    constants()
    for n in (1, 2, 3):
        cells[n].wait()
    wind_w, inv_cel, courant = tab[2, me], tab[3, me], tab[4, me]
    grow(0)
    forward(0)
    grow(1)
    forward(1)
    interact(0)
    grow(2)
    forward(2)
    interact(1)
    grow(3)
    forward(3)
    gather(0)
    interact(2)
    gather(1)
    interact(3)
    finish(0)
    gather(2)
    finish(1)
    edges()
    gather(3, 0)
    gather(3, 1)
    finish(2)
    lon_to_right().wait_recv()
    lon_to_left().wait_recv()
    propagate((0,), (0, 1))
    propagate((0,), (2, 3))
    finish(3, 0)
    propagate((1, 2, 3), (0, 1))
    finish(3, 1)
    propagate((1, 2, 3), (2,))
    propagate((1, 2, 3), (3,))

    for i in range(4):
        for dz in (1, 2, 3):
            zin(i, dz).wait_send()
        for f in halo_ups(i):
            hal_up(i, f).wait_send()
        for f in halo_dns(i):
            hal_dn(i, f).wait_send()
        for half in range(2 if i == 3 else 1):
            for dz in (1, 2, 3):
                zout(i, dz, half).wait_send()
            for m in back_ups(i):
                bak_up(i, m, half).wait_send()
            for m in back_dns(i):
                bak_dn(i, m, half).wait_send()
        for quarter in range(4):
            store(i, quarter).wait()
    lon_to_right().wait_send()
    lon_to_left().wait_send()


def shards(spectra, u_wind, wind_dir, sea_mask):
    f32 = jnp.float32
    tile = (NTH, 8, LANES)
    vmem, dma = pltpu.VMEM, pltpu.SemaphoreType.DMA
    outer = pl.BlockSpec(memory_space=pltpu.HBM)
    shape = u_wind.shape
    def stay(a):
        return pltpu.with_memory_space_constraint(a, pltpu.HBM)

    columns = jnp.transpose(spectra, (0, 2, 1, 3))
    result = pl.pallas_call(
        kernel,
        out_shape=jax.ShapeDtypeStruct(columns.shape, f32),
        in_specs=[
            outer, outer, outer, outer, outer,
        ],
        out_specs=pl.BlockSpec(memory_space=pl.ANY),
        scratch_shapes=[
            pltpu.SMEM((8, 128), f32),
            vmem(shape, f32), vmem(shape, f32), vmem(shape, jnp.int32),
            vmem((4, NTH, LAT, LANES), f32),
            vmem((4, NTH, LAT, LANES), f32),
            vmem((4, 4) + tile, f32),
            vmem((4, 12) + tile, f32),
            vmem((4, 12) + tile, f32),
            vmem((4, 4) + tile, f32),
            vmem((4, 4) + tile, f32),
            vmem((4, 4) + tile, f32),
            vmem((4, 4) + tile, f32),
            vmem((4, 4) + tile, f32),
            vmem((NTH + 2 * PAD, 8, LANES), f32),
            vmem((NTH + 2 * PAD, 8, LANES), f32),
            vmem((NTH + 2 * PAD, 8, LANES), f32),
            vmem((NTH + 2 * PAD, 8, LANES), f32),
            vmem((4,) + tile, f32),
            vmem((4,) + tile, f32),
            vmem((4,) + tile, f32),
            vmem((LAT, LANES), f32),
            vmem((LAT, LANES), f32),
            vmem((LAT, LANES), f32),
            vmem((4, 8, LANES), f32),
            vmem((4, 8, LANES), f32),
            vmem((4, 8, LANES), f32),
            vmem((4, 8, LANES), f32),
            dma((4,)), dma((16,)), dma((4,)),
            dma((16,)), dma((16,)),
            dma((32,)), dma((32,)),
            dma((40,)), dma((40,)),
            dma((20,)), dma((20,)),
            dma((2,)), dma((2,)),
        ],
        compiler_params=pltpu.CompilerParams(
            collective_id=0, has_side_effects=True, vmem_limit_bytes=50 << 20
        ),
        cost_estimate=pl.CostEstimate(flops=60_000_000, bytes_accessed=5_000_000, transcendentals=32_768),
        name="wave_step",
    )(*(stay(a) for a in (jnp.asarray(tables()), columns, u_wind, wind_dir, sea_mask)))
    return jnp.transpose(result, (0, 2, 1, 3))


def solution(mesh):
    return jax.shard_map(
        shards,
        mesh=mesh,
        in_specs=(P("comp", None, None, "grid"), P(None, "grid"), P(None, "grid"), P(None, "grid")),
        out_specs=P("comp", None, None, "grid"),
        check_vma=False,
    )
```

```python
import math

import numpy as np

import jax
import jax.numpy as jnp
from jax import lax
from jax.experimental import pallas as pl
from jax.experimental.pallas import tpu as pltpu
from jax.sharding import PartitionSpec as P

MESH = pl.DeviceIdType.MESH
NK, NTH, LAT = 32, 36, 32
GRAVITY = 9.81
LAMBDA = 0.25
WIND = 0.0003125 * 120.0
ADVECT_STEP = 220.0
EARTH_RADIUS = 6371000.0
BAND_CENTRE = 30.0
CELL_DEGREES = 0.05
CELL_RADIANS = CELL_DEGREES * math.pi / 180.0
SHIFT_UP = math.log(1.0 + LAMBDA) / math.log(1.1)
SHIFT_DOWN = math.log(1.0 - LAMBDA) / math.log(1.1)
NEAR = 11.48 * NTH / 360.0
FAR = 33.56 * NTH / 360.0
U1 = SHIFT_UP - 2.0
U0 = 1.0 - U1
D1W = -SHIFT_DOWN - 3.0
D0W = 1.0 - D1W
N1 = NEAR - 1.0
N0 = 1.0 - N1
F1 = FAR - 3.0
F0 = 1.0 - F1
W_UP = 0.1 / (1.0 + LAMBDA) ** 4
W_DOWN = 0.1 / (1.0 - LAMBDA) ** 4
W_CROSS = 0.2 / (1.0 - LAMBDA * LAMBDA) ** 4

ORDER = (0, 3, 1, 2)
WINDOW = (0, 1, 0, 1)
LANES = 128
HALF = NTH // 2
JB = 4
PAD = 4


def tables():
    t = np.zeros((8, 128), np.float64)
    th = 2.0 * np.pi * np.arange(NTH) / NTH
    t[0, :NTH] = np.cos(th)
    t[1, :NTH] = np.sin(th)
    f = 0.04 * 1.1 ** np.arange(NK)
    w = 2.0 * np.pi * f
    t[2, :NK] = WIND * w
    t[3, :NK] = w / GRAVITY
    t[4, :NK] = GRAVITY / (2.0 * w) * ADVECT_STEP / (EARTH_RADIUS * CELL_RADIANS)
    return t.astype(np.float32)


def halo_ups(i):
    return range(1, 4) if WINDOW[i] else range(4)


def halo_dns(i):
    return range(4) if WINDOW[i] else range(3)


def back_ups(i):
    return range(4) if WINDOW[i] else range(3)


def back_dns(i):
    return range(1, 4) if WINDOW[i] else range(4)


def kernel(
    tab_hbm, x_hbm, uw_hbm, wd_hbm, mk_hbm, o_hbm,
    tab, uw, wd, mk, xbuf, obuf, sbuf, ebuf, tbuf, above, below, incr, ibuf, post,
    eux, edx, d1x, d2x, bus, bds, cen, rowinv, facehi, facelo,
    pack_l, pack_r, halo_l, halo_r,
    load_s, store_s, cell_s, zin_s, zin_r, hal_s, hal_r, bak_s, bak_r, zout_s, zout_r, lon_s, lon_r,
):
    f32 = jnp.float32
    me = lax.axis_index("comp")
    g = lax.axis_index("grid")
    y, z = me // 4, lax.rem(me, 4)
    y_up = lax.rem(y + 1, 8) * 4 + z
    y_dn = lax.rem(y + 7, 8) * 4 + z
    g_right, g_left = lax.rem(g + 1, 16), lax.rem(g + 15, 16)
    has_lo = jnp.where(y > 0, 1.0, 0.0).astype(f32)
    has_hi = jnp.where(y < 7, 1.0, 0.0).astype(f32)
    has_left = jnp.where(g > 0, 1.0, 0.0).astype(f32)
    has_right = jnp.where(g < 15, 1.0, 0.0).astype(f32)

    def zpeer(dz):
        return lax.rem(z + dz, 4)

    def zfrom(dz):
        return lax.rem(z + 4 - dz, 4)

    def load(i):
        return pltpu.make_async_copy(
            x_hbm.at[0, :, :, pl.ds(ORDER[i] * LANES, LANES)], xbuf.at[i], load_s.at[i]
        )

    def store(i, quarter):
        at = pl.ds(quarter * (NTH // 4), NTH // 4)
        return pltpu.make_async_copy(
            obuf.at[i, at], o_hbm.at[0, at, :, pl.ds(ORDER[i] * LANES, LANES)], store_s.at[i * 4 + quarter]
        )

    def travels(i, f, four, action):
        if four:
            action()
        else:

            @pl.when(f >= 1 if WINDOW[i] else f < 3)
            def _():
                action()

    def halo_each(i, f, up, down):
        travels(i, f, WINDOW[i] == 0, up)
        travels(i, f, WINDOW[i] == 1, down)

    def back_each(i, m, up, down):
        travels(i, m, WINDOW[i] == 1, up)
        travels(i, m, WINDOW[i] == 0, down)

    def part(i, half):
        return pl.ds(half * HALF, HALF) if i == 3 else pl.ds(0, NTH)

    def remote(src, dst, ss, rs, **to):
        return pltpu.make_async_remote_copy(
            src_ref=src, dst_ref=dst, send_sem=ss, recv_sem=rs, device_id=to, device_id_type=MESH
        )

    def zin(i, dz):
        p = zpeer(dz)
        k = i * 4 + dz
        return remote(sbuf.at[i, p], ebuf.at[i, 4 + z], zin_s.at[k], zin_r.at[k], comp=y * 4 + p)

    def hal_up(i, f):
        k = i * 8 + f
        return remote(ebuf.at[i, 4 + f], ebuf.at[i, f], hal_s.at[k], hal_r.at[k], comp=y_up)

    def hal_dn(i, f):
        k = i * 8 + 4 + f
        return remote(ebuf.at[i, 4 + f], ebuf.at[i, 8 + f], hal_s.at[k], hal_r.at[k], comp=y_dn)

    def bak_dn(i, m, half=0):
        k, at = (i + half) * 8 + m, part(i, half)
        return remote(tbuf.at[i, m, at], above.at[i, m, at], bak_s.at[k], bak_r.at[k], comp=y_dn)

    def bak_up(i, m, half=0):
        k, at = (i + half) * 8 + 4 + m, part(i, half)
        return remote(tbuf.at[i, 8 + m, at], below.at[i, m, at], bak_s.at[k], bak_r.at[k], comp=y_up)

    def zout(i, dz, half=0):
        p, at = zpeer(dz), part(i, half)
        k = (i + half) * 4 + dz
        return remote(incr.at[i, p, at], ibuf.at[i, z, at], zout_s.at[k], zout_r.at[k], comp=y * 4 + p)

    def lon_to_right():
        return remote(pack_r, halo_l, lon_s.at[0], lon_r.at[0], grid=g_right)

    def lon_to_left():
        return remote(pack_l, halo_r, lon_s.at[1], lon_r.at[1], grid=g_left)

    cells = [
        pltpu.make_async_copy(src, dst, cell_s.at[n])
        for n, (src, dst) in enumerate(
            ((mk_hbm, mk), (uw_hbm, uw), (wd_hbm, wd), (tab_hbm, tab))
        )
    ]
    cells[0].start()
    for i in range(4):
        load(i).start()
    for n in (3, 1, 2):
        cells[n].start()

    barrier = pltpu.get_barrier_semaphore()
    for dz in (1, 2, 3):
        pl.semaphore_signal(barrier, inc=1, device_id={"comp": y * 4 + zpeer(dz)}, device_id_type=MESH)
    pl.semaphore_signal(barrier, inc=1, device_id={"comp": y_up}, device_id_type=MESH)
    pl.semaphore_signal(barrier, inc=1, device_id={"comp": y_dn}, device_id_type=MESH)
    pl.semaphore_signal(barrier, inc=1, device_id={"grid": g_right}, device_id_type=MESH)
    pl.semaphore_signal(barrier, inc=1, device_id={"grid": g_left}, device_id_type=MESH)

    def lanes(i):
        return slice(ORDER[i] * LANES, (ORDER[i] + 1) * LANES)

    def rows8(rg):
        return pl.ds(pl.multiple_of(rg * 8, 8), 8)

    def prepare(i):
        load(i).wait()
        for dz in (2, 1, 3, 0):
            rg = zpeer(dz)
            sea = mk[rows8(rg), lanes(i)].astype(f32)

            @pl.loop(0, NTH // JB)
            def _(b):
                at = pl.ds(b * JB, JB)
                piece = xbuf[i, at, rows8(rg)] * sea[None]
                sbuf[i, rg, at] = piece
                if dz == 0:
                    ebuf[i, 4 + z, at] = piece

            if i == 0 and dz == 2:
                pl.semaphore_wait(barrier, 7)
            if i == 0 and dz:
                zin(i, dz).start()
        send_halo(i, z)


    def grow(i):
        for rg in range(4):
            speed = uw[rg * 8 : rg * 8 + 8, lanes(i)] * inv_cel
            head = wd[rg * 8 : rg * 8 + 8, lanes(i)]
            along, across = speed * jnp.cos(head), speed * jnp.sin(head)

            @pl.loop(0, NTH, unroll=4)
            def _(j):
                growth = wind_w * jnp.maximum(0.0, tab[0, j] * along + tab[1, j] * across - 1.0)
                post[i, rg, j] = sbuf[i, rg, j] * (1.0 + growth)

    def constants():
        row = lax.broadcasted_iota(jnp.int32, (LAT, LANES), 0).astype(f32)

        def cosine(offset):
            return jnp.cos((BAND_CENTRE + (row - offset) * CELL_DEGREES) * (math.pi / 180.0))

        inverse = 1.0 / cosine((LAT - 1) / 2.0)
        rowinv[...] = inverse
        facehi[...] = cosine(LAT / 2.0 - 1.0) * inverse
        facelo[...] = cosine(LAT / 2.0) * inverse
        for i in range(4):
            if WINDOW[i]:
                above[i, 0] = jnp.zeros((NTH, 8, LANES), f32)
            else:
                below[i, 3] = jnp.zeros((NTH, 8, LANES), f32)

    def send_halo(i, f):
        halo_each(i, f, lambda: hal_up(i, f).start(), lambda: hal_dn(i, f).start())

    def forward(i):
        for dz in (1, 2, 3):
            zin(i, dz).wait_recv()
            if i < 3:
                zin(i + 1, dz).start()
            send_halo(i, zfrom(dz))

    def interact(i):
        for f in halo_ups(i):
            hal_up(i, f).wait_recv()
        for f in halo_dns(i):
            hal_dn(i, f).wait_recv()
        w = WINDOW[i]

        @pl.loop(0, 4)
        def _(k):
            beyond = k >= 4 - w
            low = jnp.where(beyond, has_hi, 1.0)
            lo_a = jnp.where(k < 4 - w, has_lo, low) * D1W
            lo_b = jnp.where(k < 3 - w, has_lo, low) * D0W
            hi_a = jnp.where((k >= 2 - w) & ~beyond, has_hi, 1.0) * U0
            hi_b = jnp.where((k >= 1 - w) & ~beyond, has_hi, 1.0) * U1

            @pl.loop(0, NTH // JB)
            def _(b):
                at = pl.ds(b * JB, JB)
                to = pl.ds(b * JB + PAD, JB)
                eux[to] = hi_a * ebuf[i, k + w + 6, at] + hi_b * ebuf[i, k + w + 7, at]
                edx[to] = lo_b * ebuf[i, k + w + 1, at] + lo_a * ebuf[i, k + w, at]

            for ref in (eux, edx):
                ref[0:PAD] = ref[NTH : NTH + PAD]
                ref[NTH + PAD : NTH + 2 * PAD] = ref[PAD : 2 * PAD]

            @pl.loop(0, NTH // JB)
            def _(b):
                def eu(o):
                    return eux[pl.ds(b * JB + PAD + o, JB)]

                def ed(o):
                    return edx[pl.ds(b * JB + PAD + o, JB)]

                e = ebuf[i, k + w + 4, pl.ds(b * JB, JB)]

                def delta(plus, minus):
                    return e * (e * (W_UP * plus + W_DOWN * minus) - W_CROSS * plus * minus)

                to = pl.ds(b * JB + PAD, JB)
                d1x[to] = delta(N0 * eu(1) + N1 * eu(2), F0 * ed(-3) + F1 * ed(-4))
                d2x[to] = delta(N0 * eu(-1) + N1 * eu(-2), F0 * ed(3) + F1 * ed(4))

            for ref in (d1x, d2x):
                ref[0:PAD] = ref[NTH : NTH + PAD]
                ref[NTH + PAD : NTH + 2 * PAD] = ref[PAD : 2 * PAD]

            @pl.loop(0, NTH // JB)
            def _(b):
                def a1(o):
                    return d1x[pl.ds(b * JB + PAD + o, JB)]

                def a2(o):
                    return d2x[pl.ds(b * JB + PAD + o, JB)]

                at = pl.ds(b * JB, JB)
                bus[k, at] = N0 * (a1(-1) + a2(1)) + N1 * (a1(-2) + a2(2))
                bds[k, at] = F0 * (a1(3) + a2(-3)) + F1 * (a1(4) + a2(-4))
                cen[k, at] = -2.0 * (a1(0) + a2(0))

        @pl.loop(0, NTH)
        def _(j):
            bd = [bds[k, j] for k in range(4)]
            bu = [bus[k, j] for k in range(4)]
            ce = [cen[k, j] for k in range(4)]
            if w:
                own = has_hi * bd[3]
                tbuf[i, 1, j] = D1W * bd[0]
                tbuf[i, 2, j] = D0W * bd[0] + D1W * bd[1]
                tbuf[i, 3, j] = D0W * bd[1] + D1W * bd[2]
                tbuf[i, 4, j] = D0W * bd[2] + D1W * own
                tbuf[i, 5, j] = ce[0] + D0W * own
                tbuf[i, 6, j] = ce[1]
                tbuf[i, 7, j] = ce[2] + U0 * bu[0]
                tbuf[i, 8, j] = ce[3] + has_hi * (U1 * bu[0] + U0 * bu[1])
                tbuf[i, 9, j] = has_hi * (U1 * bu[1] + U0 * bu[2])
                tbuf[i, 10, j] = has_hi * (U1 * bu[2]) + U0 * bu[3]
                tbuf[i, 11, j] = U1 * bu[3]
            else:
                tbuf[i, 0, j] = D1W * bd[0]
                tbuf[i, 1, j] = D0W * bd[0] + D1W * bd[1]
                tbuf[i, 2, j] = D0W * bd[1] + D1W * bd[2]
                tbuf[i, 3, j] = D0W * bd[2] + D1W * bd[3]
                tbuf[i, 4, j] = ce[0] + D0W * bd[3]
                tbuf[i, 5, j] = ce[1]
                tbuf[i, 6, j] = ce[2] + U0 * bu[0]
                tbuf[i, 7, j] = ce[3] + U1 * bu[0] + U0 * bu[1]
                tbuf[i, 8, j] = U1 * bu[1] + U0 * bu[2]
                tbuf[i, 9, j] = U1 * bu[2] + U0 * bu[3]
                tbuf[i, 10, j] = U1 * bu[3]

        for dz in (1, 2, 3, 0):
            m = zpeer(dz)
            back_each(i, m, lambda: bak_up(i, m).start(), lambda: bak_dn(i, m).start())

    def gather(i, half=0):
        at = part(i, half)
        for dz in (1, 2, 3, 0):
            m = zpeer(dz)
            more = i == 3 and half == 0

            def up():
                bak_up(i, m, half).wait_recv()
                if more:
                    bak_up(i, m, 1).start()

            def down():
                bak_dn(i, m, half).wait_recv()
                if more:
                    bak_dn(i, m, 1).start()

            back_each(i, m, up, down)
            under = 1.0 if WINDOW[i] else has_lo
            total = tbuf[i, 4 + m, at] + has_hi * above[i, m, at] + under * below[i, m, at]
            if dz == 0:
                ibuf[i, z, at] = total
            else:
                incr[i, m, at] = total
                zout(i, dz, half).start()

    def finish(i, half=0):
        for dz in (1, 2, 3):
            zout(i, dz, half).wait_recv()
        whole = part(i, half).size

        @pl.loop(0, whole // 6)
        def _(b):
            at = pl.ds(half * HALF + b * 6, 6)
            for rg in range(4):
                post[i, rg, at] = post[i, rg, at] + ibuf[i, rg, at]

    lane = lax.broadcasted_iota(jnp.int32, (8, LANES), 1)

    def edges():
        first, last = ORDER.index(0), ORDER.index(3)

        @pl.loop(0, 4)
        def _(rg):
            a, b = post[first, rg, 0], pltpu.roll(post[last, rg, 0], 2, 1)
            for j in range(1, NTH):
                here = lane >= 2 * j
                a = jnp.where(here, pltpu.roll(post[first, rg, j], 2 * j, 1), a)
                b = jnp.where(here, pltpu.roll(post[last, rg, j], 2 * j + 2, 1), b)
            pack_l[rg] = a
            pack_r[rg] = b

        lon_to_right().start()
        lon_to_left().start()

    sub = lax.broadcasted_iota(jnp.int32, (8, LANES), 0)

    def shift(here, other, by, axis):
        size = LANES if axis else 8
        place = lane if axis else sub
        if by > 0:
            return pltpu.roll(jnp.where(place >= size - by, other, here), by, axis)
        return pltpu.roll(jnp.where(place < -by, other, here), size + by, axis)

    def sweep_x(c, v, left, right, positive):
        c = c if positive else -c
        q = (1.0 - c * c) * (1.0 / 6.0)
        mid = 0.5 + 0.5 * c + 2.0 * q
        far = 0.5 - 0.5 * c - q
        k_next, k_here = c * far, 1.0 - c * (mid - far)
        k_back, k_back2 = c * (q + mid), c * q
        outs = []
        for here, low, high in zip(v, left, right, strict=True):
            up, dn = (low, high) if positive else (high, low)
            way = 1 if positive else -1
            nxt = shift(here, dn, -way, 1)
            back = shift(here, up, way, 1)
            back2 = shift(here, up, 2 * way, 1)
            outs.append(k_here * here - k_next * nxt + k_back * back - k_back2 * back2)
        return outs

    def sweep_y(c, u, positive):
        q = (1.0 - c * c) * (1.0 / 6.0)
        zero = jnp.zeros((8, LANES), f32)
        tiles = [zero, *u, zero]
        faces = []
        if positive:
            t_back, t_here, t_next = -q * c, c * (0.5 + 0.5 * c + 2.0 * q), c * (0.5 - 0.5 * c - q)
        else:
            t_here, t_next, t_next2 = c * (0.5 + 0.5 * c - q), c * (0.5 - 0.5 * c + 2.0 * q), -q * c
        for r in range(5):
            here = tiles[r]
            high = tiles[r + 1]
            face = t_here * here + t_next * shift(here, high, -1, 0)
            if positive:
                if r:
                    face = face + t_back * shift(here, tiles[r - 1], 1, 0)
            else:
                face = face + t_next2 * shift(here, high, -2, 0)
            faces.append(face)
        outs = []
        for r in range(4):
            over, under = faces[r + 1], shift(faces[r + 1], faces[r], 1, 0)
            at = slice(r * 8, r * 8 + 8)
            outs.append(u[r] - (facehi[at] * over - facelo[at] * under))
        return outs

    def propagate(chunks, quarters):
        @pl.loop(0, NTH // 4)
        def _(t):
            for quarter in quarters:
                j = t + 9 * quarter
                x_pos, y_pos = quarter in (0, 3), quarter in (0, 1)
                swept = [[None] * 4 for _ in chunks]
                for rg in range(4):
                    v = {col: post[ORDER.index(col), rg, j] for col in range(4)}
                    if 0 in chunks:
                        v[-1] = has_left * pltpu.roll(halo_l[rg], 126 - 2 * j, 1)
                    if 3 in chunks:
                        v[4] = has_right * pltpu.roll(halo_r[rg], LANES - 2 * j, 1)
                    outs = sweep_x(
                        (courant * tab[0, j]) * rowinv[rg * 8 : rg * 8 + 8],
                        [v[col] for col in chunks],
                        [v[col - 1] for col in chunks],
                        [v[col + 1] for col in chunks],
                        x_pos,
                    )
                    for n, out in enumerate(outs):
                        sea = mk[rg * 8 : rg * 8 + 8, lanes(ORDER.index(chunks[n]))]
                        swept[n][rg] = out * sea.astype(f32)
                for n, col in enumerate(chunks):
                    outs = sweep_y(courant * tab[1, j], swept[n], y_pos)
                    for rg in range(4):
                        at = slice(rg * 8, rg * 8 + 8)
                        sea = mk[at, lanes(ORDER.index(col))].astype(f32)
                        obuf[ORDER.index(col), j, at] = outs[rg] * sea

        for col in chunks:
            for quarter in quarters:
                store(ORDER.index(col), quarter).start()

    cells[0].wait()
    for i in range(4):
        prepare(i)
    constants()
    for n in (1, 2, 3):
        cells[n].wait()
    wind_w, inv_cel, courant = tab[2, me], tab[3, me], tab[4, me]
    grow(0)
    forward(0)
    grow(1)
    forward(1)
    interact(0)
    grow(2)
    forward(2)
    interact(1)
    grow(3)
    gather(0)
    forward(3)
    interact(2)
    gather(1)
    interact(3)
    finish(0)
    gather(2)
    finish(1)
    edges()
    gather(3, 0)
    gather(3, 1)
    finish(2)
    lon_to_right().wait_recv()
    lon_to_left().wait_recv()
    propagate((0,), (0, 1))
    propagate((0,), (2, 3))
    finish(3, 0)
    propagate((1, 2, 3), (0, 1))
    finish(3, 1)
    propagate((1, 2, 3), (2,))
    propagate((1, 2, 3), (3,))

    for i in range(4):
        for dz in (1, 2, 3):
            zin(i, dz).wait_send()
        for f in halo_ups(i):
            hal_up(i, f).wait_send()
        for f in halo_dns(i):
            hal_dn(i, f).wait_send()
        for half in range(2 if i == 3 else 1):
            for dz in (1, 2, 3):
                zout(i, dz, half).wait_send()
            for m in back_ups(i):
                bak_up(i, m, half).wait_send()
            for m in back_dns(i):
                bak_dn(i, m, half).wait_send()
        for quarter in range(4):
            store(i, quarter).wait()
    lon_to_right().wait_send()
    lon_to_left().wait_send()


def shards(spectra, u_wind, wind_dir, sea_mask):
    f32 = jnp.float32
    tile = (NTH, 8, LANES)
    vmem, dma = pltpu.VMEM, pltpu.SemaphoreType.DMA
    outer = pl.BlockSpec(memory_space=pltpu.HBM)
    shape = u_wind.shape
    def stay(a):
        return pltpu.with_memory_space_constraint(a, pltpu.HBM)

    columns = jnp.transpose(spectra, (0, 2, 1, 3))
    result = pl.pallas_call(
        kernel,
        out_shape=jax.ShapeDtypeStruct(columns.shape, f32),
        in_specs=[
            outer, outer, outer, outer, outer,
        ],
        out_specs=pl.BlockSpec(memory_space=pl.ANY),
        scratch_shapes=[
            pltpu.SMEM((8, 128), f32),
            vmem(shape, f32), vmem(shape, f32), vmem(shape, jnp.int32),
            vmem((4, NTH, LAT, LANES), f32),
            vmem((4, NTH, LAT, LANES), f32),
            vmem((4, 4) + tile, f32),
            vmem((4, 12) + tile, f32),
            vmem((4, 12) + tile, f32),
            vmem((4, 4) + tile, f32),
            vmem((4, 4) + tile, f32),
            vmem((4, 4) + tile, f32),
            vmem((4, 4) + tile, f32),
            vmem((4, 4) + tile, f32),
            vmem((NTH + 2 * PAD, 8, LANES), f32),
            vmem((NTH + 2 * PAD, 8, LANES), f32),
            vmem((NTH + 2 * PAD, 8, LANES), f32),
            vmem((NTH + 2 * PAD, 8, LANES), f32),
            vmem((4,) + tile, f32),
            vmem((4,) + tile, f32),
            vmem((4,) + tile, f32),
            vmem((LAT, LANES), f32),
            vmem((LAT, LANES), f32),
            vmem((LAT, LANES), f32),
            vmem((4, 8, LANES), f32),
            vmem((4, 8, LANES), f32),
            vmem((4, 8, LANES), f32),
            vmem((4, 8, LANES), f32),
            dma((4,)), dma((16,)), dma((4,)),
            dma((16,)), dma((16,)),
            dma((32,)), dma((32,)),
            dma((40,)), dma((40,)),
            dma((20,)), dma((20,)),
            dma((2,)), dma((2,)),
        ],
        compiler_params=pltpu.CompilerParams(
            collective_id=0, has_side_effects=True, vmem_limit_bytes=50 << 20
        ),
        cost_estimate=pl.CostEstimate(flops=60_000_000, bytes_accessed=5_000_000, transcendentals=32_768),
        name="wave_step",
    )(*(stay(a) for a in (jnp.asarray(tables()), columns, u_wind, wind_dir, sea_mask)))
    return jnp.transpose(result, (0, 2, 1, 3))


def solution(mesh):
    return jax.shard_map(
        shards,
        mesh=mesh,
        in_specs=(P("comp", None, None, "grid"), P(None, "grid"), P(None, "grid"), P(None, "grid")),
        out_specs=P("comp", None, None, "grid"),
        check_vma=False,
    )
```
